32 devices in a mesh: sec: 4 (over x, core), fsdp: 8 (over z, y).
Axes of the slice: x: 2, y: 2, z: 4, core: 2. Of those that a mesh axis runs over, the one named last changes fastest.
Arguments:
- tokens: bfloat16 [4096, 6144], P('fsdp', 'sec'), may hold values from -6 to 6
- grad_out: bfloat16 [4096, 6144], P('fsdp', 'sec'), may hold values from -6 to 6
- gain: float32 [6144], P('sec'), may hold values from 0.1 to 7
- qkv_weight: bfloat16 [6144, 384], P(('sec', 'fsdp')), may hold values from -0.078125 to 0.078125
- out_weight: bfloat16 [128, 6144], P(None, ('sec', 'fsdp')), may hold values from -0.5 to 0.5
Outputs:
- grad_tokens: bfloat16 [4096, 6144], P('fsdp', 'sec')
- grad_qkv: float32 [6144, 384], P(('sec', 'fsdp'))
- grad_outw: float32 [128, 6144], P(None, ('sec', 'fsdp'))
- grad_gain: float32 [6144], P(('sec', 'fsdp'))
The draws below stay inside these ranges and needn't reach their ends.
All inputs are finite; a program needn't handle non-finite values.
Results may differ from the reference program's by a relative error of at most 0.012.
The reference program's roundings to bfloat16 on the way (of `hidden`, `proj`, `probs_b`, `attended`, `grad_att`, `grad_score` and `grad_proj`) count: a program that leaves them out, or rounds other values in their place, can miss the bound.
Values may be sent and summed in bfloat16 or wider, within the bound.
A program may use at most 64 MiB of HBM per device.

```python
import jax
import jax.numpy as jnp
from jax import lax

D = 6144
HD = 128
PATCHES = 256
IMAGES = 16
TOKENS = 4096


def draw_gain(key, part):
    position = jnp.arange(D, dtype=jnp.float32) / (D - 1)
    base = jnp.exp(jnp.log(0.4) + jnp.log(10.0) * position)
    rough = jax.random.uniform(key, (D,), jnp.float32, 0.7, 1.3)
    return (base * rough).astype(jnp.float32)


def strengthened(drawn, stream_key, source, target, shards_of, factor):
    def block_of(axis_at):
        return (jnp.arange(drawn.shape[axis_at]) // (drawn.shape[axis_at] // shards_of)).reshape((-1,) + (1,) * (drawn.ndim - 1 - axis_at))

    one_side = jax.random.permutation(stream_key, shards_of)[block_of(target)]
    far = (block_of(target) + shards_of // 2) % shards_of
    return jnp.where((block_of(source) == one_side) | (block_of(source) == far), factor * drawn, drawn)


def shard_levels(key, dims, split, smallest, largest):
    level = 1.0
    for dim, shards_of in split:
        steps = jax.random.uniform(jax.random.fold_in(jax.random.fold_in(key, 6), dim), (shards_of,), jnp.float32, smallest / len(split), largest / len(split))
        level = level * jnp.repeat(jnp.exp(steps), dims[dim] // shards_of).reshape((-1,) + (1,) * (len(dims) - 1 - dim))
    return level


def noise(own_key, extent, deviation, bound, split=(), kind=jnp.bfloat16):
    result = deviation * jax.random.normal(own_key, extent, jnp.float32)
    if split:
        result = result * shard_levels(own_key, extent, split, -0.22, 0.18)
    return jnp.clip(result, -bound, bound).astype(kind)


def noise_with(stream_key, dims, width, most, pieces, heavy, kind=jnp.bfloat16):
    entries = width * jax.random.normal(stream_key, dims, jnp.float32)
    if pieces:
        entries = entries * shard_levels(stream_key, dims, pieces, -0.22, 0.18)
    return jnp.clip(strengthened(entries, jax.random.fold_in(stream_key, 3), *heavy), -most, most).astype(kind)


def setup_inputs(seed: int = 0) -> dict:
    keys = jax.random.split(jax.random.key(seed), 6)
    return {
        "tokens": noise(keys[0], (TOKENS, D), 1.0, 6.0, ((0, 8), (1, 4))),
        "grad_out": noise_with(keys[1], (TOKENS, D), 1.0, 6.0, ((0, 8), (1, 4)), (0, 1, 8, 2.0)),
        "gain": draw_gain(jax.random.fold_in(keys[5], 71), 0),
        "qkv_weight": noise(keys[3], (D, 3 * HD), D ** -0.5, 0.078125, ((0, 32),)),
        "out_weight": noise(keys[4], (HD, D), HD ** -0.5, 0.5, ((1, 32),)),
    }


EPS = 1e-06

def reference(tokens, grad_out, gain, qkv_weight, out_weight):
    tok_float = tokens.astype(jnp.float32)
    row_mean = lax.optimization_barrier(jnp.sum(tok_float, axis=1)) / D
    row_var = lax.optimization_barrier(jnp.sum(tok_float * tok_float, axis=1)) / D - row_mean * row_mean
    inv_std = lax.rsqrt(row_var + EPS)
    normed = (tok_float - row_mean[:, None]) * inv_std[:, None]
    hidden = (normed * gain[None, :]).astype(jnp.bfloat16)
    proj = jnp.dot(hidden, qkv_weight, preferred_element_type=jnp.float32).astype(jnp.bfloat16)
    parts = proj.reshape(IMAGES, PATCHES, 3, HD).astype(jnp.float32)
    query, key_in, value = (parts[:, :, 0], parts[:, :, 1], parts[:, :, 2])
    scale = 1.0 / HD ** 0.5
    scores = jnp.einsum('ipd,iqd->ipq', query, key_in) * scale
    probs = jax.nn.softmax(scores, axis=-1)
    probs_b = probs.astype(jnp.bfloat16)
    attended = jnp.einsum('ipq,iqd->ipd', probs_b.astype(jnp.float32), value).astype(jnp.bfloat16)
    attended = attended.reshape(TOKENS, HD)
    grad_outw = jnp.dot(attended.T, grad_out, preferred_element_type=jnp.float32)
    grad_att = jnp.dot(grad_out, out_weight.T, preferred_element_type=jnp.float32).astype(jnp.bfloat16)
    grad_att3 = grad_att.reshape(IMAGES, PATCHES, HD).astype(jnp.float32)
    grad_prob = jnp.einsum('ipd,iqd->ipq', grad_att3, value)
    grad_score = (probs * (grad_prob - lax.optimization_barrier(jnp.sum(grad_prob * probs, axis=-1, keepdims=True))) * scale).astype(jnp.bfloat16)
    score_f = grad_score.astype(jnp.float32)
    grad_query = jnp.einsum('ipq,iqd->ipd', score_f, key_in)
    grad_key = jnp.einsum('ipq,ipd->iqd', score_f, query)
    grad_value = jnp.einsum('ipq,ipd->iqd', probs_b.astype(jnp.float32), grad_att3)
    grad_proj = jnp.stack([grad_query, grad_key, grad_value], axis=2).reshape(TOKENS, 3 * HD).astype(jnp.bfloat16)
    grad_qkv = jnp.dot(hidden.T, grad_proj, preferred_element_type=jnp.float32)
    grad_hidden = jnp.dot(grad_proj, qkv_weight.T, preferred_element_type=jnp.float32)
    grad_gain = lax.optimization_barrier(jnp.sum(grad_hidden * normed, axis=0))
    grad_normed = grad_hidden * gain[None, :]
    first = lax.optimization_barrier(jnp.sum(grad_normed, axis=1)) / D
    second = lax.optimization_barrier(jnp.sum(grad_normed * normed, axis=1)) / D
    grad_tokens = grad_out.astype(jnp.float32) + inv_std[:, None] * (grad_normed - first[:, None] - normed * second[:, None])
    return (grad_tokens.astype(jnp.bfloat16), grad_qkv, grad_outw, grad_gain)
```

```python
import functools

import jax
import jax.numpy as jnp
from jax import lax
from jax.experimental import pallas as pl
from jax.experimental.pallas import tpu as pltpu
from jax.sharding import PartitionSpec as P

PATCHES = 256
EPS = 1e-06
MESH = pl.DeviceIdType.MESH
F32 = jnp.float32
BF16 = jnp.bfloat16


def nn(a, b):
    return jnp.dot(a, b, preferred_element_type=F32)


def nt(a, b):
    return lax.dot_general(a, b, (((1,), (1,)), ((), ())), preferred_element_type=F32)


def tn(a, b):
    return lax.dot_general(a, b, (((0,), (0,)), ((), ())), preferred_element_type=F32)


def copy_to(src, dst, send, recv, device):
    return pltpu.make_async_remote_copy(
        src_ref=src,
        dst_ref=dst,
        send_sem=send,
        recv_sem=recv,
        device_id=device,
        device_id_type=MESH,
    )


def kernel(
    nz,
    width,
    tok_ref,
    go_ref,
    gain_ref,
    qkv_ref,
    ow_ref,
    gt_ref,
    grad_ref,
    weights,
    hidden,
    hidden_t,
    go_t,
    stats,
    mean_inv,
    first_out,
    first_own,
    first_in,
    second_out,
    second_in,
    gp,
    moments,
    sums,
    y_out,
    y_in,
    own,
    left_out,
    right_out,
    left_in,
    right_in,
    gather_send,
    gather_recv,
    stat_send,
    stat_recv,
    core_send,
    core_recv,
    x_send,
    x_recv,
    gp_send,
    gp_recv,
    y_send,
    y_recv,
    chain_send,
    chain_recv,
):
    rows, local = tok_ref.shape
    depth, head = ow_ref.shape
    groups = weights.shape[0]
    half = rows // 2
    s = lax.axis_index("sec")
    f = lax.axis_index("fsdp")
    z, y = f // 2, f % 2
    c = s % 2
    core = {"sec": s + 1 - 2 * c}
    across = {"sec": (s + 2) % 4}
    other_y = {"fsdp": f + 1 - 2 * y}
    to_left = {"fsdp": f - 2}
    to_right = {"fsdp": f + 2}
    has_left = z > 0
    has_right = z < nz - 1

    barrier = pltpu.get_barrier_semaphore()

    def greet(device):
        pl.semaphore_signal(barrier, inc=1, device_id=device, device_id_type=MESH)

    greet(other_y)
    for k in range(1, 4):
        greet({"sec": (s + k) % 4})
    pl.when(has_left)(lambda: greet(to_left))
    pl.when(has_right)(lambda: greet(to_right))

    mine = pl.ds(pl.multiple_of(f * depth, depth), depth)
    weights[0, mine, :] = ow_ref[...]
    for g in range(1, groups):
        weights[g, mine, :] = qkv_ref[:, (g - 1) * head : g * head]

    peers = 4 + has_left.astype(jnp.int32) + has_right.astype(jnp.int32)
    pl.semaphore_wait(barrier, peers)

    def block(g, shard):
        return weights.at[g, pl.ds(pl.multiple_of(shard * depth, depth), depth), :]

    def gather_copy(g, shard_z, way, device):
        shard = shard_z * 2 + y
        ref = block(g, shard)
        return copy_to(
            ref, ref, gather_send.at[g, way, shard_z], gather_recv.at[g, shard], device
        )

    def go_left(g, shard_z):
        return gather_copy(g, shard_z, 0, to_left)

    def go_right(g, shard_z):
        return gather_copy(g, shard_z, 1, to_right)

    def go_y(g, shard_z):
        return gather_copy(g, shard_z, 2, other_y)

    def arrived(g, shard):
        ref = block(g, shard)
        copy_to(
            ref, ref, gather_send.at[g, 0, 0], gather_recv.at[g, shard], other_y
        ).wait_recv()

    def send_own(g):
        pl.when(has_left)(lambda: go_left(g, z).start())
        pl.when(has_right)(lambda: go_right(g, z).start())
        go_y(g, z).start()

    def forward(g):
        for d in range(1, nz):

            @pl.when(z - d >= 0)
            def _():
                arrived(g, (z - d) * 2 + y)
                pl.when(has_right)(lambda: go_right(g, z - d).start())
                go_y(g, z - d).start()

            @pl.when(z + d < nz)
            def _():
                arrived(g, (z + d) * 2 + y)
                pl.when(has_left)(lambda: go_left(g, z + d).start())
                go_y(g, z + d).start()

    def gathered(g):
        for shard_z in range(nz):
            arrived(g, shard_z * 2 + 1 - y)

    def gather_sent():
        for g in range(groups):
            for shard_z in range(nz):
                pl.when(has_left & (z <= shard_z))(lambda: go_left(g, shard_z).wait_send())
                pl.when(has_right & (z >= shard_z))(lambda: go_right(g, shard_z).wait_send())
                go_y(g, shard_z).wait_send()

    send_own(0)
    send_own(1)

    step = 64
    lane = lax.broadcasted_iota(jnp.int32, (step, 128), 1)

    def row_sums(i, carry):
        r = pl.ds(pl.multiple_of(i * step, step), step)
        t = tok_ref[r, :].astype(F32)
        a = jnp.sum(t, axis=1, keepdims=True)
        b = jnp.sum(t * t, axis=1, keepdims=True)
        mean_inv[r, :] = jnp.where(lane == 0, a, b)
        return carry

    lax.fori_loop(0, rows // step, row_sums, 0)
    stats[s] = mean_inv[...].T[:8, :]

    def stat_copy(k):
        return copy_to(
            stats.at[s], stats.at[s], stat_send.at[k], stat_recv.at[s], {"sec": (s + k) % 4}
        )

    for k in range(1, 4):
        stat_copy(k).start()

    forward(0)
    send_own(2)

    tstep = 256

    def turn(src, dst):
        for i in range(rows // tstep):

            def body(j, carry):
                cols = pl.ds(pl.multiple_of(j * tstep, tstep), tstep)
                part = src[i * tstep : (i + 1) * tstep, cols].astype(F32)
                dst[cols, i * tstep : (i + 1) * tstep] = part.T.astype(BF16)
                return carry

            lax.fori_loop(0, local // tstep, body, 0)

    turn(go_ref, go_t)

    gain_row = gain_ref[...]
    g_hi = gain_row.astype(BF16)
    rest = gain_row - g_hi.astype(F32)
    g_mid = rest.astype(BF16)
    g_lo = (rest - g_mid.astype(F32)).astype(BF16)
    row16 = lax.broadcasted_iota(jnp.int32, (16, local), 0)
    gain16 = jnp.where(
        row16 == 0,
        g_hi.astype(F32),
        jnp.where(row16 == 1, g_mid.astype(F32), jnp.where(row16 == 2, g_lo.astype(F32), 0.0)),
    ).astype(BF16)

    my_rows = pl.ds(pl.multiple_of(c * half, half), half)
    their_rows = pl.ds(pl.multiple_of((1 - c) * half, half), half)

    def core_copy(g):
        return copy_to(
            first_out.at[g], first_in.at[g], core_send.at[g], core_recv.at[g], core
        )

    def x_copy(g):
        return copy_to(
            second_out.at[g], second_in.at[g], x_send.at[g], x_recv.at[g], across
        )

    def project(g, left):
        w = weights[g]
        u = jnp.sum(nn(gain16, w), axis=0, keepdims=True)
        u = jnp.broadcast_to(u, (8, head))
        first_out[g, half : half + 8, :] = u
        first_out[g, 0:half, :] = nn(left[their_rows, :], w)
        core_copy(g).start()
        first_own[g, half : half + 8, :] = u
        first_own[g, 0:half, :] = nn(left[my_rows, :], w)

    def across_start(g):
        core_copy(g).wait_recv()
        second_out[g] = first_own[g] + first_in[g]
        x_copy(g).start()

    gathered(0)
    project(0, go_ref)
    forward(1)
    send_own(3)

    for k in range(1, 4):
        sender = (s + k) % 4
        copy_to(
            stats.at[sender], stats.at[sender], stat_send.at[k], stat_recv.at[sender], core
        ).wait_recv()
    total = stats[0] + stats[1] + stats[2] + stats[3]
    row_mean = total[0:1, :] / width
    row_var = total[1:2, :] / width - row_mean * row_mean
    inv_std = lax.rsqrt(row_var + EPS)
    sub = lax.broadcasted_iota(jnp.int32, (128, rows), 0)
    mean_inv[...] = jnp.where(sub == 0, row_mean, inv_std).T

    def norm(i, carry):
        r = pl.ds(pl.multiple_of(i * step, step), step)
        t = tok_ref[r, :].astype(F32)
        m = mean_inv[r, :]
        normed = (t - m[:, 0:1]) * m[:, 1:2]
        hidden[r, :] = (normed * gain_ref[...]).astype(BF16)
        return carry

    lax.fori_loop(0, rows // step, norm, 0)

    across_start(0)
    gathered(1)
    project(1, hidden)
    forward(2)
    across_start(1)
    gathered(2)
    project(2, hidden)
    forward(3)
    across_start(2)
    turn(hidden, hidden_t)
    gathered(3)
    project(3, hidden)
    across_start(3)

    def finish(g):
        x_copy(g).wait_recv()
        sums[g] = second_out[g] + second_in[g]

    for g in range(groups):
        finish(g)

    scale = 1.0 / head**0.5
    grad_att = sums[0, 0:half, :].astype(BF16)
    query = sums[1, 0:half, :].astype(BF16)
    key = sums[2, 0:half, :].astype(BF16)
    value = sums[3, 0:half, :].astype(BF16)
    scores = nt(query, key) * scale
    e = jnp.exp(scores - jnp.max(scores, axis=-1, keepdims=True))
    probs = e / jnp.sum(e, axis=-1, keepdims=True)
    probs_b = probs.astype(BF16)
    gp[my_rows, 0:head] = nn(probs_b, value).astype(BF16)

    def gp_copy(k):
        ref = (
            gp.at[my_rows, pl.ds(0, head)],
            gp.at[my_rows, pl.ds(head, 3 * head)],
            moments.at[my_rows, :],
        )[k]
        return copy_to(ref, ref, gp_send.at[k], gp_recv.at[k], core)

    def gp_arrived(k):
        ref = (
            gp.at[their_rows, pl.ds(0, head)],
            gp.at[their_rows, pl.ds(head, 3 * head)],
            moments.at[their_rows, :],
        )[k]
        copy_to(ref, ref, gp_send.at[k], gp_recv.at[k], core).wait_recv()

    gp_copy(0).start()
    grad_prob = nt(grad_att, value)
    grad_score = (
        probs * (grad_prob - jnp.sum(grad_prob * probs, axis=-1, keepdims=True)) * scale
    ).astype(BF16)

    spans = (slice(0, head), slice(head, 4 * head))
    turned = (go_t, hidden_t)
    order = []
    for k in range(nz):
        order.append(nz - 1 - k // 2 if k % 2 == 0 else k // 2)

    def part(p, shard):
        r = pl.ds(pl.multiple_of(shard * depth, depth), depth)
        return nn(turned[p][r, :], gp[:, spans[p]])

    def y_copy(p, shard_z):
        cols = pl.ds(spans[p].start, spans[p].stop - spans[p].start)
        return copy_to(
            y_out.at[shard_z, :, cols],
            y_in.at[shard_z, :, cols],
            y_send.at[p, shard_z],
            y_recv.at[p, shard_z],
            other_y,
        )

    def y_phase(p):
        for shard_z in order:
            y_out[shard_z, :, spans[p]] = part(p, shard_z * 2 + 1 - y).astype(BF16)
            y_copy(p, shard_z).start()

    def own_phase(p):
        for shard_z in order:
            own[shard_z, :, spans[p]] = part(p, shard_z * 2 + y)

    gp_arrived(0)
    y_phase(0)

    grad_query = nn(grad_score, key)
    grad_key = tn(grad_score, query)
    grad_value = tn(probs_b, grad_att)
    lane_h = lax.broadcasted_iota(jnp.int32, (half, 128), 1)
    first = jnp.zeros((half, 1), F32)
    second = jnp.zeros((half, 1), F32)
    for g, grad in enumerate((grad_query, grad_key, grad_value)):
        rounded = grad.astype(BF16)
        gp[my_rows, (g + 1) * head : (g + 2) * head] = rounded
        r32 = rounded.astype(F32)
        u = sums[g + 1, half : half + 1, :]
        first += jnp.sum(r32 * u, axis=1, keepdims=True)
        second += jnp.sum(r32 * sums[g + 1, 0:half, :], axis=1, keepdims=True)
    moments[my_rows, :] = jnp.where(lane_h == 0, first, second) / width
    gp_copy(1).start()
    gp_copy(2).start()
    own_phase(0)
    gp_arrived(1)
    y_phase(1)
    own_phase(1)

    tile = 256
    gp_arrived(2)

    def token_tile(j):
        cols = pl.ds(pl.multiple_of(j * tile, tile), tile)
        grad_hidden = nt(gp[:, head : 2 * head], weights[1, cols, :])
        for g in range(2, groups):
            grad_hidden += nt(gp[:, g * head : (g + 1) * head], weights[g, cols, :])
        m = mean_inv[...]
        inv = m[:, 1:2]
        normed = (tok_ref[:, cols].astype(F32) - m[:, 0:1]) * inv
        mo = moments[...]
        grad_normed = grad_hidden * gain_ref[:, cols]
        gt_ref[:, cols] = (
            go_ref[:, cols].astype(F32)
            + inv * (grad_normed - mo[:, 0:1] - normed * mo[:, 1:2])
        ).astype(BF16)

    def chain_copy(p, way, dest):
        cols = pl.ds(spans[p].start, spans[p].stop - spans[p].start)
        out, into, device = ((left_out, left_in, to_left), (right_out, right_in, to_right))[way]
        return copy_to(
            out.at[dest, :, cols],
            into.at[dest, :, cols],
            chain_send.at[p, way, dest],
            chain_recv.at[p, way, dest],
            device,
        )

    steps = []
    for k in range(nz - 1):
        steps += [(1, nz - 1 - k), (0, k)]

    def chain(p, between):
        span = spans[p]
        for way, dest in steps:
            out, into = ((left_out, left_in), (right_out, right_in))[way]
            passes = (z > dest) if way == 0 else (z < dest)
            follows = has_right if way == 0 else has_left
            between()

            @pl.when(passes)
            def _():
                y_copy(p, dest).wait_recv()
                here = own[dest, :, span] + y_in[dest, :, span].astype(F32)

                @pl.when(follows)
                def _():
                    chain_copy(p, way, dest).wait_recv()
                    out[dest, :, span] = (here + into[dest, :, span].astype(F32)).astype(BF16)

                @pl.when(jnp.logical_not(follows))
                def _():
                    out[dest, :, span] = here.astype(BF16)

                chain_copy(p, way, dest).start()

    def chain_end(p):
        span = spans[p]
        y_copy(p, z).wait_recv()
        grad_ref[:, span] = own[z, :, span] + y_in[z, :, span].astype(F32)

        @pl.when(has_left)
        def _():
            chain_copy(p, 1, z).wait_recv()
            grad_ref[:, span] += right_in[z, :, span].astype(F32)

        @pl.when(has_right)
        def _():
            chain_copy(p, 0, z).wait_recv()
            grad_ref[:, span] += left_in[z, :, span].astype(F32)

    tiles = iter(range(local // tile))

    def between():
        j = next(tiles, None)
        if j is not None:
            token_tile(j)

    chain(0, lambda: None)
    chain(1, between)
    for j in tiles:
        token_tile(j)
    chain_end(0)
    chain_end(1)

    gather_sent()
    for k in range(1, 4):
        stat_copy(k).wait_send()
    for g in range(groups):
        core_copy(g).wait_send()
        x_copy(g).wait_send()
    for k in range(3):
        gp_copy(k).wait_send()
    for p in range(2):
        for shard_z in range(nz):
            y_copy(p, shard_z).wait_send()
        for way, dest in steps:
            passes = (z > dest) if way == 0 else (z < dest)
            pl.when(passes)(lambda: chain_copy(p, way, dest).wait_send())


def fused(nz, width, tokens, grad_out, gain, qkv_weight, out_weight):
    rows, local = tokens.shape
    head = out_weight.shape[0]
    depth = qkv_weight.shape[0]
    half = rows // 2
    n = 2 * nz
    vmem = pl.BlockSpec(memory_space=pltpu.VMEM)
    dma = pltpu.SemaphoreType.DMA
    exchange = pltpu.VMEM((4, half + 8, head), F32)
    pieces = pltpu.VMEM((nz, depth, 4 * head), BF16)
    return pl.pallas_call(
        functools.partial(kernel, nz, width),
        out_shape=(
            jax.ShapeDtypeStruct((rows, local), BF16),
            jax.ShapeDtypeStruct((depth, 4 * head), F32),
        ),
        in_specs=[vmem] * 5,
        out_specs=(vmem, vmem),
        scratch_shapes=[
            pltpu.VMEM((4, local, head), BF16),
            pltpu.VMEM((rows, local), BF16),
            pltpu.VMEM((local, rows), BF16),
            pltpu.VMEM((local, rows), BF16),
            pltpu.VMEM((4, 8, rows), F32),
            pltpu.VMEM((rows, 128), F32),
            exchange,
            exchange,
            exchange,
            exchange,
            exchange,
            pltpu.VMEM((rows, 4 * head), BF16),
            pltpu.VMEM((rows, 128), F32),
            exchange,
            pieces,
            pieces,
            pltpu.VMEM((nz, depth, 4 * head), F32),
            pieces,
            pieces,
            pieces,
            pieces,
            dma((4, 3, nz)),
            dma((4, n)),
            dma((4,)),
            dma((4,)),
            dma((4,)),
            dma((4,)),
            dma((4,)),
            dma((4,)),
            dma((3,)),
            dma((3,)),
            dma((2, nz)),
            dma((2, nz)),
            dma((2, 2, nz)),
            dma((2, 2, nz)),
        ],
        compiler_params=pltpu.CompilerParams(
            collective_id=0, has_side_effects=True, vmem_limit_bytes=48 * 1024 * 1024
        ),
        name="head_backward",
    )(tokens, grad_out, gain.reshape(1, local), qkv_weight, out_weight.T)


def on_device(tokens, grad_out, gain, qkv_weight, out_weight):
    tok_rows, local_width = tokens.shape
    model_width = local_width * lax.axis_size("sec")
    head_size = out_weight.shape[0]
    shards = lax.axis_size("fsdp")
    depth = qkv_weight.shape[0]
    if depth % 64 or tok_rows != 2 * PATCHES or lax.axis_size("sec") != 4 or shards % 2:
        return by_collectives(tokens, grad_out, gain, qkv_weight, out_weight)
    grad_tokens, grads = fused(
        shards // 2, model_width, tokens, grad_out, gain, qkv_weight, out_weight
    )
    grad_qkv = grads[:, head_size:]
    grad_outw = grads[:, :head_size].T
    own_gain = lax.dynamic_slice_in_dim(gain, lax.axis_index("fsdp") * depth, depth)
    grad_gain = jnp.sum(qkv_weight.astype(F32) * grad_qkv, axis=1) / own_gain
    return grad_tokens, grad_qkv, grad_outw, grad_gain


def by_collectives(tokens, grad_out, gain, qkv_weight, out_weight):
    tok_rows, local_width = tokens.shape
    model_width = local_width * lax.axis_size("sec")
    head_size = out_weight.shape[0]
    images = tok_rows // PATCHES
    tok_float = tokens.astype(jnp.float32)
    row_sums, row_squares = lax.psum(
        (jnp.sum(tok_float, axis=1), jnp.sum(tok_float * tok_float, axis=1)), "sec"
    )
    row_mean = row_sums / model_width
    row_var = row_squares / model_width - row_mean * row_mean
    inv_std = lax.rsqrt(row_var + EPS)
    normed = (tok_float - row_mean[:, None]) * inv_std[:, None]
    hidden = (normed * gain[None, :]).astype(jnp.bfloat16)
    columns = hidden
    partial_value = jnp.dot(
        columns,
        lax.all_gather(qkv_weight, "fsdp", axis=0, tiled=True),
        preferred_element_type=jnp.float32,
    )
    proj = lax.psum(partial_value, "sec").astype(jnp.bfloat16)
    parts = proj.reshape(images, PATCHES, 3, head_size)
    query, key_in, value = (parts[:, :, 0], parts[:, :, 1], parts[:, :, 2])
    scale = 1.0 / head_size**0.5
    scores = jnp.einsum("ipd,iqd->ipq", query, key_in, preferred_element_type=jnp.float32) * scale
    probs = jax.nn.softmax(scores, axis=-1)
    probs_b = probs.astype(jnp.bfloat16)
    attended = jnp.einsum(
        "ipq,iqd->ipd", probs_b, value, preferred_element_type=jnp.float32
    ).astype(jnp.bfloat16)
    attended = attended.reshape(tok_rows, head_size)
    local_outw = lax.dot_general(
        attended, grad_out, (((0,), (0,)), ((), ())), preferred_element_type=jnp.float32
    )
    grad_outw = lax.psum_scatter(local_outw, "fsdp", scatter_dimension=1, tiled=True)
    columns = grad_out
    att_partial = lax.dot_general(
        columns,
        lax.all_gather(out_weight, "fsdp", axis=1, tiled=True),
        (((1,), (1,)), ((), ())),
        preferred_element_type=jnp.float32,
    )
    grad_att = lax.psum(att_partial, "sec").astype(jnp.bfloat16)
    grad_att3 = grad_att.reshape(images, PATCHES, head_size)
    grad_prob = jnp.einsum("ipd,iqd->ipq", grad_att3, value, preferred_element_type=jnp.float32)
    grad_score = (
        probs * (grad_prob - jnp.sum(grad_prob * probs, axis=-1, keepdims=True)) * scale
    ).astype(jnp.bfloat16)
    grad_query = jnp.einsum("ipq,iqd->ipd", grad_score, key_in, preferred_element_type=jnp.float32)
    grad_key = jnp.einsum("ipq,ipd->iqd", grad_score, query, preferred_element_type=jnp.float32)
    grad_value = jnp.einsum("ipq,ipd->iqd", probs_b, grad_att3, preferred_element_type=jnp.float32)
    grad_proj = (
        jnp.stack([grad_query, grad_key, grad_value], axis=2)
        .reshape(tok_rows, 3 * head_size)
        .astype(jnp.bfloat16)
    )
    local_qkv = lax.dot_general(
        hidden, grad_proj, (((0,), (0,)), ((), ())), preferred_element_type=jnp.float32
    )
    grad_hidden = lax.dot_general(
        grad_proj,
        lax.all_gather(qkv_weight, "fsdp", axis=0, tiled=True),
        (((1,), (1,)), ((), ())),
        preferred_element_type=jnp.float32,
    )
    local_gain = jnp.sum(grad_hidden * normed, axis=0)
    grad_normed = grad_hidden * gain[None, :]
    first_sum, second_sum = lax.psum(
        (jnp.sum(grad_normed, axis=1), jnp.sum(grad_normed * normed, axis=1)), "sec"
    )
    first = first_sum / model_width
    second = second_sum / model_width
    grad_tokens = grad_out.astype(jnp.float32) + inv_std[:, None] * (
        grad_normed - first[:, None] - normed * second[:, None]
    )
    grad_qkv, grad_gain = (
        lax.psum_scatter(local_qkv, "fsdp", scatter_dimension=0, tiled=True),
        lax.psum_scatter(local_gain, "fsdp", scatter_dimension=0, tiled=True),
    )
    return (grad_tokens.astype(jnp.bfloat16), grad_qkv, grad_outw, grad_gain)


def solution(mesh):
    placed = (
        P("fsdp", "sec"),
        P("fsdp", "sec"),
        P("sec"),
        P(("sec", "fsdp"), None),
        P(None, ("sec", "fsdp")),
    )
    return jax.shard_map(
        on_device,
        mesh=mesh,
        in_specs=placed,
        out_specs=(
            P("fsdp", "sec"),
            P(("sec", "fsdp"), None),
            P(None, ("sec", "fsdp")),
            P(("sec", "fsdp")),
        ),
        check_vma=False,
    )
```

```python
import functools

import jax
import jax.numpy as jnp
from jax import lax
from jax.experimental import pallas as pl
from jax.experimental.pallas import tpu as pltpu
from jax.sharding import PartitionSpec as P

PATCHES = 256
EPS = 1e-06
MESH = pl.DeviceIdType.MESH
F32 = jnp.float32
BF16 = jnp.bfloat16


def nn(a, b):
    return jnp.dot(a, b, preferred_element_type=F32)


def nt(a, b):
    return lax.dot_general(a, b, (((1,), (1,)), ((), ())), preferred_element_type=F32)


def tn(a, b):
    return lax.dot_general(a, b, (((0,), (0,)), ((), ())), preferred_element_type=F32)


def copy_to(src, dst, send, recv, device):
    return pltpu.make_async_remote_copy(
        src_ref=src,
        dst_ref=dst,
        send_sem=send,
        recv_sem=recv,
        device_id=device,
        device_id_type=MESH,
    )


def kernel(
    nz,
    width,
    tok_hbm,
    go_hbm,
    gain_ref,
    qkv_hbm,
    ow_hbm,
    gt_ref,
    grad_ref,
    ggain_ref,
    tok_ref,
    go_ref,
    weights,
    hidden,
    hidden_t,
    go_t,
    gain_t,
    gain_pad,
    stats,
    mean_inv,
    first_out,
    first_own,
    first_in,
    second_out,
    second_in,
    gp,
    moments,
    sums,
    y_out,
    y_in,
    own,
    chain_out,
    chain_in,
    load_sem,
    gather_send,
    gather_recv,
    stat_send,
    stat_recv,
    core_send,
    core_recv,
    x_send,
    x_recv,
    gp_send,
    gp_recv,
    y_send,
    y_recv,
    chain_send,
    chain_recv,
):
    rows, local = tok_ref.shape
    depth, head = ow_hbm.shape
    groups = weights.shape[0]
    half = rows // 2
    s = lax.axis_index("sec")
    f = lax.axis_index("fsdp")
    z, y = f // 2, f % 2
    c = s % 2
    core = {"sec": s + 1 - 2 * c}
    across = {"sec": (s + 2) % 4}
    other_y = {"fsdp": f + 1 - 2 * y}
    to_left = {"fsdp": f - 2}
    to_right = {"fsdp": f + 2}
    has_left = z > 0
    has_right = z < nz - 1

    barrier = pltpu.get_barrier_semaphore()

    def greet(device):
        pl.semaphore_signal(barrier, inc=1, device_id=device, device_id_type=MESH)

    greet(other_y)
    for k in range(1, 4):
        greet({"sec": (s + k) % 4})
    pl.when(has_left)(lambda: greet(to_left))
    pl.when(has_right)(lambda: greet(to_right))

    mine = pl.ds(pl.multiple_of(f * depth, depth), depth)
    loads = [pltpu.make_async_copy(ow_hbm, weights.at[0, mine, :], load_sem.at[0])]
    for g in range(1, groups):
        part_hbm = qkv_hbm.at[:, pl.ds((g - 1) * head, head)]
        loads.append(pltpu.make_async_copy(part_hbm, weights.at[g, mine, :], load_sem.at[g]))
    loads.append(pltpu.make_async_copy(tok_hbm, tok_ref, load_sem.at[4]))
    loads.append(pltpu.make_async_copy(go_hbm, go_ref, load_sem.at[5]))
    for load in loads:
        load.start()

    peers = 4 + has_left.astype(jnp.int32) + has_right.astype(jnp.int32)
    pl.semaphore_wait(barrier, peers)

    def block(g, shard):
        return weights.at[g, pl.ds(pl.multiple_of(shard * depth, depth), depth), :]

    def gather_copy(g, shard_z, way, device):
        shard = shard_z * 2 + y
        ref = block(g, shard)
        return copy_to(
            ref, ref, gather_send.at[g, way, shard_z], gather_recv.at[g, shard], device
        )

    def go_left(g, shard_z):
        return gather_copy(g, shard_z, 0, to_left)

    def go_right(g, shard_z):
        return gather_copy(g, shard_z, 1, to_right)

    def go_y(g, shard_z):
        return gather_copy(g, shard_z, 2, other_y)

    def arrived(g, shard):
        ref = block(g, shard)
        copy_to(
            ref, ref, gather_send.at[g, 0, 0], gather_recv.at[g, shard], other_y
        ).wait_recv()

    def send_own(g):
        pl.when(has_left)(lambda: go_left(g, z).start())
        pl.when(has_right)(lambda: go_right(g, z).start())
        go_y(g, z).start()

    def forward(g):
        for d in range(1, nz):

            @pl.when(z - d >= 0)
            def _():
                arrived(g, (z - d) * 2 + y)
                pl.when(has_right)(lambda: go_right(g, z - d).start())
                go_y(g, z - d).start()

            @pl.when(z + d < nz)
            def _():
                arrived(g, (z + d) * 2 + y)
                pl.when(has_left)(lambda: go_left(g, z + d).start())
                go_y(g, z + d).start()

    def gathered(g):
        for shard_z in range(nz):
            arrived(g, shard_z * 2 + 1 - y)

    def gather_sent():
        for g in range(groups):
            for shard_z in range(nz):
                pl.when(has_left & (z <= shard_z))(lambda: go_left(g, shard_z).wait_send())
                pl.when(has_right & (z >= shard_z))(lambda: go_right(g, shard_z).wait_send())
                go_y(g, shard_z).wait_send()

    loads[0].wait()
    send_own(0)
    loads[1].wait()
    send_own(1)
    loads[4].wait()

    step = 64
    lane = lax.broadcasted_iota(jnp.int32, (step, 128), 1)

    def row_sums(i, carry):
        r = pl.ds(pl.multiple_of(i * step, step), step)
        t = tok_ref[r, :].astype(F32)
        a = jnp.sum(t, axis=1, keepdims=True)
        b = jnp.sum(t * t, axis=1, keepdims=True)
        mean_inv[r, :] = jnp.where(lane == 0, a, b)
        return carry

    lax.fori_loop(0, rows // step, row_sums, 0)
    stats[s] = mean_inv[...].T[:8, :]

    def stat_copy(k):
        return copy_to(
            stats.at[s], stats.at[s], stat_send.at[k], stat_recv.at[s], {"sec": (s + k) % 4}
        )

    for k in range(1, 4):
        stat_copy(k).start()

    forward(0)
    loads[2].wait()
    send_own(2)
    loads[3].wait()
    loads[5].wait()

    tstep = 256

    def turn(src, dst):
        for i in range(rows // tstep):

            def body(j, carry):
                cols = pl.ds(pl.multiple_of(j * tstep, tstep), tstep)
                part = src[i * tstep : (i + 1) * tstep, cols].astype(F32)
                dst[cols, i * tstep : (i + 1) * tstep] = part.T.astype(BF16)
                return carry

            lax.fori_loop(0, local // tstep, body, 0)

    turn(go_ref, go_t)
    forward(1)
    send_own(3)
    gain_t[...] = jnp.broadcast_to(gain_ref[...], (128, local)).T

    gain_row = gain_ref[...]
    g_hi = gain_row.astype(BF16)
    rest = gain_row - g_hi.astype(F32)
    g_mid = rest.astype(BF16)
    g_lo = (rest - g_mid.astype(F32)).astype(BF16)
    row16 = lax.broadcasted_iota(jnp.int32, (16, local), 0)
    gain16 = jnp.where(
        row16 == 0,
        g_hi.astype(F32),
        jnp.where(row16 == 1, g_mid.astype(F32), jnp.where(row16 == 2, g_lo.astype(F32), 0.0)),
    ).astype(BF16)

    my_rows = pl.ds(pl.multiple_of(c * half, half), half)
    their_rows = pl.ds(pl.multiple_of((1 - c) * half, half), half)

    def core_copy(g):
        return copy_to(
            first_out.at[g], first_in.at[g], core_send.at[g], core_recv.at[g], core
        )

    def x_copy(g):
        return copy_to(
            second_out.at[g], second_in.at[g], x_send.at[g], x_recv.at[g], across
        )

    def project(g, left):
        w = weights[g]
        u = jnp.sum(nn(gain16, w), axis=0, keepdims=True)
        u = jnp.broadcast_to(u, (8, head))
        first_out[g, half : half + 8, :] = u
        first_out[g, 0:half, :] = nn(left[their_rows, :], w)
        core_copy(g).start()
        first_own[g, half : half + 8, :] = u
        first_own[g, 0:half, :] = nn(left[my_rows, :], w)

    def across_start(g):
        core_copy(g).wait_recv()
        second_out[g] = first_own[g] + first_in[g]
        x_copy(g).start()

    gathered(0)
    project(0, go_ref)

    for k in range(1, 4):
        sender = (s + k) % 4
        copy_to(
            stats.at[sender], stats.at[sender], stat_send.at[k], stat_recv.at[sender], core
        ).wait_recv()
    total = stats[0] + stats[1] + stats[2] + stats[3]
    row_mean = total[0:1, :] / width
    row_var = total[1:2, :] / width - row_mean * row_mean
    inv_std = lax.rsqrt(row_var + EPS)
    sub = lax.broadcasted_iota(jnp.int32, (128, rows), 0)
    mean_inv[...] = jnp.where(sub == 0, row_mean, inv_std).T

    def norm(i, carry):
        r = pl.ds(pl.multiple_of(i * step, step), step)
        t = tok_ref[r, :].astype(F32)
        m = mean_inv[r, :]
        normed = (t - m[:, 0:1]) * m[:, 1:2]
        hidden[r, :] = (normed * gain_ref[...]).astype(BF16)
        return carry

    lax.fori_loop(0, rows // step, norm, 0)

    across_start(0)
    forward(2)
    gathered(1)
    project(1, hidden)
    forward(3)
    across_start(1)
    gathered(2)
    project(2, hidden)
    turn(hidden, hidden_t)
    across_start(2)
    gathered(3)
    project(3, hidden)
    across_start(3)

    def finish(g):
        x_copy(g).wait_recv()
        sums[g] = second_out[g] + second_in[g]
        return sums[g, 0:half, :].astype(BF16)

    scale = 1.0 / head**0.5
    grad_att = finish(0)
    query = finish(1)
    key = finish(2)
    scores = nt(query, key) * scale
    e = jnp.exp(scores - jnp.max(scores, axis=-1, keepdims=True))
    probs = e / jnp.sum(e, axis=-1, keepdims=True)
    probs_b = probs.astype(BF16)

    def gp_piece(k, r):
        return moments.at[r, :] if k == groups else gp.at[r, pl.ds(k * head, head)]

    def gp_copy(k):
        ref = gp_piece(k, my_rows)
        return copy_to(ref, ref, gp_send.at[k], gp_recv.at[k], core)

    def gp_arrived(k):
        ref = gp_piece(k, their_rows)
        copy_to(ref, ref, gp_send.at[k], gp_recv.at[k], core).wait_recv()

    def gp_put(k, result):
        rounded = result.astype(BF16)
        gp[my_rows, k * head : (k + 1) * head] = rounded
        gp_copy(k).start()
        return rounded

    grad_value = gp_put(3, tn(probs_b, grad_att))
    value = finish(3)
    gp_put(0, nn(probs_b, value))
    grad_prob = nt(grad_att, value)
    grad_score = (
        probs * (grad_prob - jnp.sum(grad_prob * probs, axis=-1, keepdims=True)) * scale
    ).astype(BF16)
    grad_query = gp_put(1, nn(grad_score, key))
    grad_key = gp_put(2, tn(grad_score, query))
    lane_h = lax.broadcasted_iota(jnp.int32, (half, 128), 1)
    first = jnp.zeros((half, 1), F32)
    second = jnp.zeros((half, 1), F32)
    for g, grad in ((1, grad_query), (2, grad_key), (3, grad_value)):
        r32 = grad.astype(F32)
        u = sums[g, half : half + 1, :]
        first += jnp.sum(r32 * u, axis=1, keepdims=True)
        second += jnp.sum(r32 * sums[g, 0:half, :], axis=1, keepdims=True)
    moments[my_rows, :] = jnp.where(lane_h == 0, first, second) / width
    gp_copy(groups).start()

    def span(g):
        return slice(g * head, (g + 1) * head)

    def cols_of(g):
        return pl.ds(g * head, head)

    near = (z < nz // 2).astype(jnp.int32)

    def far_end(way, k):
        return way * (nz - 1 - k) + (1 - way) * k

    def part(g, shard):
        r = pl.ds(pl.multiple_of(shard * depth, depth), depth)
        return nn((go_t if g == 0 else hidden_t)[r, :], gp[:, span(g)])

    def y_copy(g, shard_z):
        return copy_to(
            y_out.at[shard_z, :, cols_of(g)],
            y_in.at[shard_z, :, cols_of(g)],
            y_send.at[g, shard_z],
            y_recv.at[g, shard_z],
            other_y,
        )

    def y_phase(g):
        gp_arrived(g)
        for k in range(nz):
            shard_z = far_end(near, k)
            y_out[shard_z, :, span(g)] = part(g, shard_z * 2 + 1 - y).astype(BF16)
            y_copy(g, shard_z).start()

    def own_phase(g):
        for k in range(nz):
            own[k, :, span(g)] = part(g, k * 2 + y)

    def chain_copy(g, way, dest):
        return copy_to(
            chain_out.at[way, dest, :, cols_of(g)],
            chain_in.at[way, dest, :, cols_of(g)],
            chain_send.at[g, way, dest],
            chain_recv.at[g, way, dest],
            {"fsdp": f + 4 * way - 2},
        )

    def chain(g):
        for way in (near, 1 - near):
            follows = ((way == 1) & has_left) | ((way == 0) & has_right)
            for k in range(nz - 1):
                dest = far_end(way, k)
                passes = ((way == 1) & (dest > z)) | ((way == 0) & (dest < z))

                @pl.when(passes)
                def _():
                    y_copy(g, dest).wait_recv()
                    here = own[dest, :, span(g)] + y_in[dest, :, span(g)].astype(F32)

                    @pl.when(follows)
                    def _():
                        chain_copy(g, way, dest).wait_recv()
                        chain_out[way, dest, :, span(g)] = (
                            here + chain_in[way, dest, :, span(g)].astype(F32)
                        ).astype(BF16)

                    @pl.when(jnp.logical_not(follows))
                    def _():
                        chain_out[way, dest, :, span(g)] = here.astype(BF16)

                    chain_copy(g, way, dest).start()

    def chain_end(g):
        y_copy(g, z).wait_recv()
        grad_ref[:, span(g)] = own[z, :, span(g)] + y_in[z, :, span(g)].astype(F32)

        @pl.when(has_left)
        def _():
            chain_copy(g, 1, z).wait_recv()
            grad_ref[:, span(g)] += chain_in[1, z, :, span(g)].astype(F32)

        @pl.when(has_right)
        def _():
            chain_copy(g, 0, z).wait_recv()
            grad_ref[:, span(g)] += chain_in[0, z, :, span(g)].astype(F32)

        if g == 0:
            return 0.0
        held = weights[g, mine, :].astype(F32)
        return jnp.sum(held * grad_ref[:, span(g)], axis=1, keepdims=True)

    tile = 256

    def token_tile(j):
        cols = pl.ds(pl.multiple_of(j * tile, tile), tile)
        grad_hidden = nt(gp[:, head : 2 * head], weights[1, cols, :])
        for g in range(2, groups):
            grad_hidden += nt(gp[:, g * head : (g + 1) * head], weights[g, cols, :])
        m = mean_inv[...]
        inv = m[:, 1:2]
        normed = (tok_ref[:, cols].astype(F32) - m[:, 0:1]) * inv
        mo = moments[...]
        grad_normed = grad_hidden * gain_ref[:, cols]
        gt_ref[:, cols] = (
            go_ref[:, cols].astype(F32)
            + inv * (grad_normed - mo[:, 0:1] - normed * mo[:, 1:2])
        ).astype(BF16)

    tiles = local // tile
    for g in (0, 3, 1, 2):
        y_phase(g)
    own_phase(0)
    chain(0)
    own_phase(3)
    gp_arrived(groups)
    for j in range(tiles // 2):
        token_tile(j)
    chain(3)
    chain_end(0)
    own_phase(1)
    for j in range(tiles // 2, tiles):
        token_tile(j)
    chain(1)
    own_phase(2)
    gain_sum = chain_end(3)
    chain(2)
    gain_sum += chain_end(1)
    gain_sum += chain_end(2)
    gain_pad[...] = jnp.zeros_like(gain_pad)
    gain_pad[0:depth, :] = gain_sum / gain_t[mine, :]
    ggain_ref[...] = gain_pad[...].T[0:1, 0:depth]

    gather_sent()
    for k in range(1, 4):
        stat_copy(k).wait_send()
    for g in range(groups):
        core_copy(g).wait_send()
        x_copy(g).wait_send()
    for k in range(groups + 1):
        gp_copy(k).wait_send()
    for g in range(groups):
        for k in range(nz):
            y_copy(g, k).wait_send()
            pl.when(z > k)(lambda: chain_copy(g, 0, k).wait_send())
            pl.when(z < k)(lambda: chain_copy(g, 1, k).wait_send())


def fused(nz, width, tokens, grad_out, gain, qkv_weight, out_weight):
    rows, local = tokens.shape
    head = out_weight.shape[0]
    depth = qkv_weight.shape[0]
    half = rows // 2
    n = 2 * nz
    vmem = pl.BlockSpec(memory_space=pltpu.VMEM)
    hbm = pl.BlockSpec(memory_space=pl.ANY)
    dma = pltpu.SemaphoreType.DMA
    exchange = pltpu.VMEM((4, half + 8, head), F32)
    pieces = pltpu.VMEM((nz, depth, 4 * head), BF16)
    return pl.pallas_call(
        functools.partial(kernel, nz, width),
        out_shape=(
            jax.ShapeDtypeStruct((rows, local), BF16),
            jax.ShapeDtypeStruct((depth, 4 * head), F32),
            jax.ShapeDtypeStruct((1, depth), F32),
        ),
        in_specs=[hbm, hbm, vmem, hbm, hbm],
        out_specs=(vmem, vmem, vmem),
        scratch_shapes=[
            pltpu.VMEM((rows, local), BF16),
            pltpu.VMEM((rows, local), BF16),
            pltpu.VMEM((4, local, head), BF16),
            pltpu.VMEM((rows, local), BF16),
            pltpu.VMEM((local, rows), BF16),
            pltpu.VMEM((local, rows), BF16),
            pltpu.VMEM((local, 128), F32),
            pltpu.VMEM((-(-depth // 128) * 128, 128), F32),
            pltpu.VMEM((4, 8, rows), F32),
            pltpu.VMEM((rows, 128), F32),
            exchange,
            exchange,
            exchange,
            exchange,
            exchange,
            pltpu.VMEM((rows, 4 * head), BF16),
            pltpu.VMEM((rows, 128), F32),
            exchange,
            pieces,
            pieces,
            pltpu.VMEM((nz, depth, 4 * head), F32),
            pltpu.VMEM((2, nz, depth, 4 * head), BF16),
            pltpu.VMEM((2, nz, depth, 4 * head), BF16),
            dma((6,)),
            dma((4, 3, nz)),
            dma((4, n)),
            dma((4,)),
            dma((4,)),
            dma((4,)),
            dma((4,)),
            dma((4,)),
            dma((4,)),
            dma((5,)),
            dma((5,)),
            dma((4, nz)),
            dma((4, nz)),
            dma((4, 2, nz)),
            dma((4, 2, nz)),
        ],
        compiler_params=pltpu.CompilerParams(
            collective_id=0, has_side_effects=True, vmem_limit_bytes=58 * 1024 * 1024
        ),
        name="head_backward",
    )(tokens, grad_out, gain.reshape(1, local), qkv_weight, out_weight.T)


def on_device(tokens, grad_out, gain, qkv_weight, out_weight):
    tok_rows, local_width = tokens.shape
    model_width = local_width * lax.axis_size("sec")
    head_size = out_weight.shape[0]
    shards = lax.axis_size("fsdp")
    depth = qkv_weight.shape[0]
    if depth % 64 or tok_rows != 2 * PATCHES or lax.axis_size("sec") != 4 or shards % 2:
        return by_collectives(tokens, grad_out, gain, qkv_weight, out_weight)
    grad_tokens, grads, grad_gain = fused(
        shards // 2, model_width, tokens, grad_out, gain, qkv_weight, out_weight
    )
    return grad_tokens, grads[:, head_size:], grads[:, :head_size].T, grad_gain.reshape(depth)


def by_collectives(tokens, grad_out, gain, qkv_weight, out_weight):
    tok_rows, local_width = tokens.shape
    model_width = local_width * lax.axis_size("sec")
    head_size = out_weight.shape[0]
    images = tok_rows // PATCHES
    tok_float = tokens.astype(jnp.float32)
    row_sums, row_squares = lax.psum(
        (jnp.sum(tok_float, axis=1), jnp.sum(tok_float * tok_float, axis=1)), "sec"
    )
    row_mean = row_sums / model_width
    row_var = row_squares / model_width - row_mean * row_mean
    inv_std = lax.rsqrt(row_var + EPS)
    normed = (tok_float - row_mean[:, None]) * inv_std[:, None]
    hidden = (normed * gain[None, :]).astype(jnp.bfloat16)
    columns = hidden
    partial_value = jnp.dot(
        columns,
        lax.all_gather(qkv_weight, "fsdp", axis=0, tiled=True),
        preferred_element_type=jnp.float32,
    )
    proj = lax.psum(partial_value, "sec").astype(jnp.bfloat16)
    parts = proj.reshape(images, PATCHES, 3, head_size)
    query, key_in, value = (parts[:, :, 0], parts[:, :, 1], parts[:, :, 2])
    scale = 1.0 / head_size**0.5
    scores = jnp.einsum("ipd,iqd->ipq", query, key_in, preferred_element_type=jnp.float32) * scale
    probs = jax.nn.softmax(scores, axis=-1)
    probs_b = probs.astype(jnp.bfloat16)
    attended = jnp.einsum(
        "ipq,iqd->ipd", probs_b, value, preferred_element_type=jnp.float32
    ).astype(jnp.bfloat16)
    attended = attended.reshape(tok_rows, head_size)
    local_outw = lax.dot_general(
        attended, grad_out, (((0,), (0,)), ((), ())), preferred_element_type=jnp.float32
    )
    grad_outw = lax.psum_scatter(local_outw, "fsdp", scatter_dimension=1, tiled=True)
    columns = grad_out
    att_partial = lax.dot_general(
        columns,
        lax.all_gather(out_weight, "fsdp", axis=1, tiled=True),
        (((1,), (1,)), ((), ())),
        preferred_element_type=jnp.float32,
    )
    grad_att = lax.psum(att_partial, "sec").astype(jnp.bfloat16)
    grad_att3 = grad_att.reshape(images, PATCHES, head_size)
    grad_prob = jnp.einsum("ipd,iqd->ipq", grad_att3, value, preferred_element_type=jnp.float32)
    grad_score = (
        probs * (grad_prob - jnp.sum(grad_prob * probs, axis=-1, keepdims=True)) * scale
    ).astype(jnp.bfloat16)
    grad_query = jnp.einsum("ipq,iqd->ipd", grad_score, key_in, preferred_element_type=jnp.float32)
    grad_key = jnp.einsum("ipq,ipd->iqd", grad_score, query, preferred_element_type=jnp.float32)
    grad_value = jnp.einsum("ipq,ipd->iqd", probs_b, grad_att3, preferred_element_type=jnp.float32)
    grad_proj = (
        jnp.stack([grad_query, grad_key, grad_value], axis=2)
        .reshape(tok_rows, 3 * head_size)
        .astype(jnp.bfloat16)
    )
    local_qkv = lax.dot_general(
        hidden, grad_proj, (((0,), (0,)), ((), ())), preferred_element_type=jnp.float32
    )
    grad_hidden = lax.dot_general(
        grad_proj,
        lax.all_gather(qkv_weight, "fsdp", axis=0, tiled=True),
        (((1,), (1,)), ((), ())),
        preferred_element_type=jnp.float32,
    )
    local_gain = jnp.sum(grad_hidden * normed, axis=0)
    grad_normed = grad_hidden * gain[None, :]
    first_sum, second_sum = lax.psum(
        (jnp.sum(grad_normed, axis=1), jnp.sum(grad_normed * normed, axis=1)), "sec"
    )
    first = first_sum / model_width
    second = second_sum / model_width
    grad_tokens = grad_out.astype(jnp.float32) + inv_std[:, None] * (
        grad_normed - first[:, None] - normed * second[:, None]
    )
    grad_qkv, grad_gain = (
        lax.psum_scatter(local_qkv, "fsdp", scatter_dimension=0, tiled=True),
        lax.psum_scatter(local_gain, "fsdp", scatter_dimension=0, tiled=True),
    )
    return (grad_tokens.astype(jnp.bfloat16), grad_qkv, grad_outw, grad_gain)


def solution(mesh):
    placed = (
        P("fsdp", "sec"),
        P("fsdp", "sec"),
        P("sec"),
        P(("sec", "fsdp"), None),
        P(None, ("sec", "fsdp")),
    )
    return jax.shard_map(
        on_device,
        mesh=mesh,
        in_specs=placed,
        out_specs=(
            P("fsdp", "sec"),
            P(("sec", "fsdp"), None),
            P(None, ("sec", "fsdp")),
            P(("sec", "fsdp")),
        ),
        check_vma=False,
    )
```

```python
import functools

import jax
import jax.numpy as jnp
from jax import lax
from jax.experimental import pallas as pl
from jax.experimental.pallas import tpu as pltpu
from jax.sharding import PartitionSpec as P

PATCHES = 256
EPS = 1e-06
MESH = pl.DeviceIdType.MESH
F32 = jnp.float32
BF16 = jnp.bfloat16


def nn(a, b):
    return jnp.dot(a, b, preferred_element_type=F32)


def nt(a, b):
    return lax.dot_general(a, b, (((1,), (1,)), ((), ())), preferred_element_type=F32)


def tn(a, b):
    return lax.dot_general(a, b, (((0,), (0,)), ((), ())), preferred_element_type=F32)


def copy_to(src, dst, send, recv, device):
    return pltpu.make_async_remote_copy(
        src_ref=src,
        dst_ref=dst,
        send_sem=send,
        recv_sem=recv,
        device_id=device,
        device_id_type=MESH,
    )


def kernel(
    nz,
    width,
    tok_hbm,
    go_hbm,
    gain_ref,
    qkv_hbm,
    ow_hbm,
    gt_ref,
    grad_ref,
    ggain_ref,
    tok_ref,
    go_ref,
    weights,
    hidden,
    hidden_t,
    go_t,
    gain_t,
    gain_pad,
    stats,
    mean_inv,
    first_out,
    first_own,
    first_in,
    second_out,
    second_in,
    gp,
    moments,
    sums,
    y_out,
    y_in,
    own,
    chain_out,
    chain_in,
    load_sem,
    gather_send,
    gather_recv,
    stat_send,
    stat_recv,
    core_send,
    core_recv,
    x_send,
    x_recv,
    gp_send,
    gp_recv,
    y_send,
    y_recv,
    chain_send,
    chain_recv,
):
    rows, local = tok_ref.shape
    depth, head = ow_hbm.shape
    groups = weights.shape[0]
    half = rows // 2
    s = lax.axis_index("sec")
    f = lax.axis_index("fsdp")
    z, y = f // 2, f % 2
    c = s % 2
    core = {"sec": s + 1 - 2 * c}
    across = {"sec": (s + 2) % 4}
    other_y = {"fsdp": f + 1 - 2 * y}
    to_left = {"fsdp": f - 2}
    to_right = {"fsdp": f + 2}
    has_left = z > 0
    has_right = z < nz - 1

    barrier = pltpu.get_barrier_semaphore()

    def greet(device):
        pl.semaphore_signal(barrier, inc=1, device_id=device, device_id_type=MESH)

    greet(other_y)
    for k in range(1, 4):
        greet({"sec": (s + k) % 4})
    pl.when(has_left)(lambda: greet(to_left))
    pl.when(has_right)(lambda: greet(to_right))

    mine = pl.ds(pl.multiple_of(f * depth, depth), depth)
    loads = [pltpu.make_async_copy(ow_hbm, weights.at[0, mine, :], load_sem.at[0])]
    for g in range(1, groups):
        part_hbm = qkv_hbm.at[:, pl.ds((g - 1) * head, head)]
        loads.append(pltpu.make_async_copy(part_hbm, weights.at[g, mine, :], load_sem.at[g]))
    loads.append(pltpu.make_async_copy(tok_hbm, tok_ref, load_sem.at[4]))
    loads.append(pltpu.make_async_copy(go_hbm, go_ref, load_sem.at[5]))
    for load in loads:
        load.start()

    peers = 4 + has_left.astype(jnp.int32) + has_right.astype(jnp.int32)
    pl.semaphore_wait(barrier, peers)

    def block(g, shard):
        return weights.at[g, pl.ds(pl.multiple_of(shard * depth, depth), depth), :]

    def gather_copy(g, shard_z, way, device):
        shard = shard_z * 2 + y
        ref = block(g, shard)
        return copy_to(
            ref, ref, gather_send.at[g, way, shard_z], gather_recv.at[g, shard], device
        )

    def go_left(g, shard_z):
        return gather_copy(g, shard_z, 0, to_left)

    def go_right(g, shard_z):
        return gather_copy(g, shard_z, 1, to_right)

    def go_y(g, shard_z):
        return gather_copy(g, shard_z, 2, other_y)

    def arrived(g, shard):
        ref = block(g, shard)
        copy_to(
            ref, ref, gather_send.at[g, 0, 0], gather_recv.at[g, shard], other_y
        ).wait_recv()

    def send_own(g):
        pl.when(has_left)(lambda: go_left(g, z).start())
        pl.when(has_right)(lambda: go_right(g, z).start())
        go_y(g, z).start()

    def forward(g):
        for d in range(1, nz):

            @pl.when(z - d >= 0)
            def _():
                arrived(g, (z - d) * 2 + y)
                pl.when(has_right)(lambda: go_right(g, z - d).start())
                go_y(g, z - d).start()

            @pl.when(z + d < nz)
            def _():
                arrived(g, (z + d) * 2 + y)
                pl.when(has_left)(lambda: go_left(g, z + d).start())
                go_y(g, z + d).start()

    def gathered(g):
        for shard_z in range(nz):
            arrived(g, shard_z * 2 + 1 - y)

    def gather_sent():
        for g in range(groups):
            for shard_z in range(nz):
                pl.when(has_left & (z <= shard_z))(lambda: go_left(g, shard_z).wait_send())
                pl.when(has_right & (z >= shard_z))(lambda: go_right(g, shard_z).wait_send())
                go_y(g, shard_z).wait_send()

    loads[1].wait()
    send_own(1)
    loads[2].wait()
    send_own(2)
    loads[4].wait()

    step = 64
    lane = lax.broadcasted_iota(jnp.int32, (step, 128), 1)

    def row_sums(i, carry):
        r = pl.ds(pl.multiple_of(i * step, step), step)
        t = tok_ref[r, :].astype(F32)
        a = jnp.sum(t, axis=1, keepdims=True)
        b = jnp.sum(t * t, axis=1, keepdims=True)
        mean_inv[r, :] = jnp.where(lane == 0, a, b)
        return carry

    lax.fori_loop(0, rows // step, row_sums, 0)
    stats[s] = mean_inv[...].T[:8, :]

    def stat_copy(k):
        return copy_to(
            stats.at[s], stats.at[s], stat_send.at[k], stat_recv.at[s], {"sec": (s + k) % 4}
        )

    for k in range(1, 4):
        stat_copy(k).start()

    forward(1)
    loads[3].wait()
    send_own(3)
    loads[0].wait()
    loads[5].wait()

    tstep = 256

    def turn(src, dst):
        for i in range(rows // tstep):

            def body(j, carry):
                cols = pl.ds(pl.multiple_of(j * tstep, tstep), tstep)
                part = src[i * tstep : (i + 1) * tstep, cols].astype(F32)
                dst[cols, i * tstep : (i + 1) * tstep] = part.T.astype(BF16)
                return carry

            lax.fori_loop(0, local // tstep, body, 0)


    gain_row = gain_ref[...]
    g_hi = gain_row.astype(BF16)
    rest = gain_row - g_hi.astype(F32)
    g_mid = rest.astype(BF16)
    g_lo = (rest - g_mid.astype(F32)).astype(BF16)
    row16 = lax.broadcasted_iota(jnp.int32, (16, local), 0)
    gain16 = jnp.where(
        row16 == 0,
        g_hi.astype(F32),
        jnp.where(row16 == 1, g_mid.astype(F32), jnp.where(row16 == 2, g_lo.astype(F32), 0.0)),
    ).astype(BF16)

    my_rows = pl.ds(pl.multiple_of(c * half, half), half)
    their_rows = pl.ds(pl.multiple_of((1 - c) * half, half), half)

    def core_copy(g):
        return copy_to(
            first_out.at[g], first_in.at[g], core_send.at[g], core_recv.at[g], core
        )

    def x_copy(g):
        return copy_to(
            second_out.at[g], second_in.at[g], x_send.at[g], x_recv.at[g], across
        )

    def project(g, left):
        w = weights[g]
        u = jnp.sum(nn(gain16, w), axis=0, keepdims=True)
        u = jnp.broadcast_to(u, (8, head))
        first_out[g, half : half + 8, :] = u
        first_out[g, 0:half, :] = nn(left[their_rows, :], w)
        core_copy(g).start()
        first_own[g, half : half + 8, :] = u
        first_own[g, 0:half, :] = nn(left[my_rows, :], w)

    def across_start(g):
        core_copy(g).wait_recv()
        second_out[g] = first_own[g] + first_in[g]
        x_copy(g).start()


    for k in range(1, 4):
        sender = (s + k) % 4
        copy_to(
            stats.at[sender], stats.at[sender], stat_send.at[k], stat_recv.at[sender], core
        ).wait_recv()
    total = stats[0] + stats[1] + stats[2] + stats[3]
    row_mean = total[0:1, :] / width
    row_var = total[1:2, :] / width - row_mean * row_mean
    inv_std = lax.rsqrt(row_var + EPS)
    sub = lax.broadcasted_iota(jnp.int32, (128, rows), 0)
    mean_inv[...] = jnp.where(sub == 0, row_mean, inv_std).T

    def norm(i, carry):
        r = pl.ds(pl.multiple_of(i * step, step), step)
        t = tok_ref[r, :].astype(F32)
        m = mean_inv[r, :]
        normed = (t - m[:, 0:1]) * m[:, 1:2]
        hidden[r, :] = (normed * gain_ref[...]).astype(BF16)
        return carry

    lax.fori_loop(0, rows // step, norm, 0)

    forward(2)
    send_own(0)
    turn(go_ref, go_t)
    gathered(1)
    project(1, hidden)
    forward(3)
    across_start(1)
    turn(hidden, hidden_t)
    gathered(2)
    project(2, hidden)
    forward(0)
    across_start(2)
    gathered(3)
    project(3, hidden)
    gain_t[...] = jnp.broadcast_to(gain_ref[...], (128, local)).T
    across_start(3)
    gathered(0)
    project(0, go_ref)

    def finish(g):
        x_copy(g).wait_recv()
        sums[g] = second_out[g] + second_in[g]
        return sums[g, 0:half, :].astype(BF16)

    scale = 1.0 / head**0.5
    query = finish(1)
    key = finish(2)
    scores = nt(query, key) * scale
    e = jnp.exp(scores - jnp.max(scores, axis=-1, keepdims=True))
    probs = e / jnp.sum(e, axis=-1, keepdims=True)
    probs_b = probs.astype(BF16)
    across_start(0)

    def gp_piece(k, r):
        return moments.at[r, :] if k == groups else gp.at[r, pl.ds(k * head, head)]

    def gp_copy(k):
        ref = gp_piece(k, my_rows)
        return copy_to(ref, ref, gp_send.at[k], gp_recv.at[k], core)

    def gp_arrived(k):
        ref = gp_piece(k, their_rows)
        copy_to(ref, ref, gp_send.at[k], gp_recv.at[k], core).wait_recv()

    def gp_put(k, result):
        rounded = result.astype(BF16)
        gp[my_rows, k * head : (k + 1) * head] = rounded
        gp_copy(k).start()
        return rounded

    value = finish(3)
    gp_put(0, nn(probs_b, value))

    def span(g):
        return slice(g * head, (g + 1) * head)

    def cols_of(g):
        return pl.ds(g * head, head)

    near = (z < nz // 2).astype(jnp.int32)

    def far_end(way, k):
        return way * (nz - 1 - k) + (1 - way) * k

    def part(g, shard):
        r = pl.ds(pl.multiple_of(shard * depth, depth), depth)
        return nn((go_t if g == 0 else hidden_t)[r, :], gp[:, span(g)])

    def y_copy(g, shard_z):
        return copy_to(
            y_out.at[shard_z, :, cols_of(g)],
            y_in.at[shard_z, :, cols_of(g)],
            y_send.at[g, shard_z],
            y_recv.at[g, shard_z],
            other_y,
        )

    def y_phase(g):
        gp_arrived(g)
        for k in range(nz):
            shard_z = far_end(near, k)
            y_out[shard_z, :, span(g)] = part(g, shard_z * 2 + 1 - y).astype(BF16)
            y_copy(g, shard_z).start()

    def own_phase(g):
        for k in range(nz):
            own[k, :, span(g)] = part(g, k * 2 + y)

    def chain_copy(g, way, dest):
        return copy_to(
            chain_out.at[way, dest, :, cols_of(g)],
            chain_in.at[way, dest, :, cols_of(g)],
            chain_send.at[g, way, dest],
            chain_recv.at[g, way, dest],
            {"fsdp": f + 4 * way - 2},
        )

    def chain(g):
        for way in (near, 1 - near):
            follows = ((way == 1) & has_left) | ((way == 0) & has_right)
            for k in range(nz - 1):
                dest = far_end(way, k)
                passes = ((way == 1) & (dest > z)) | ((way == 0) & (dest < z))

                @pl.when(passes)
                def _():
                    y_copy(g, dest).wait_recv()
                    here = own[dest, :, span(g)] + y_in[dest, :, span(g)].astype(F32)

                    @pl.when(follows)
                    def _():
                        chain_copy(g, way, dest).wait_recv()
                        chain_out[way, dest, :, span(g)] = (
                            here + chain_in[way, dest, :, span(g)].astype(F32)
                        ).astype(BF16)

                    @pl.when(jnp.logical_not(follows))
                    def _():
                        chain_out[way, dest, :, span(g)] = here.astype(BF16)

                    chain_copy(g, way, dest).start()

    def chain_end(g):
        y_copy(g, z).wait_recv()
        grad_ref[:, span(g)] = own[z, :, span(g)] + y_in[z, :, span(g)].astype(F32)

        @pl.when(has_left)
        def _():
            chain_copy(g, 1, z).wait_recv()
            grad_ref[:, span(g)] += chain_in[1, z, :, span(g)].astype(F32)

        @pl.when(has_right)
        def _():
            chain_copy(g, 0, z).wait_recv()
            grad_ref[:, span(g)] += chain_in[0, z, :, span(g)].astype(F32)

        if g == 0:
            return 0.0
        held = weights[g, mine, :].astype(F32)
        return jnp.sum(held * grad_ref[:, span(g)], axis=1, keepdims=True)

    y_phase(0)
    own_phase(0)

    grad_att = finish(0)
    grad_value = gp_put(3, tn(probs_b, grad_att))
    grad_prob = nt(grad_att, value)
    grad_score = (
        probs * (grad_prob - jnp.sum(grad_prob * probs, axis=-1, keepdims=True)) * scale
    ).astype(BF16)
    grad_query = gp_put(1, nn(grad_score, key))
    grad_key = gp_put(2, tn(grad_score, query))
    lane_h = lax.broadcasted_iota(jnp.int32, (half, 128), 1)
    first = jnp.zeros((half, 1), F32)
    second = jnp.zeros((half, 1), F32)
    for g, grad in ((1, grad_query), (2, grad_key), (3, grad_value)):
        r32 = grad.astype(F32)
        u = sums[g, half : half + 1, :]
        first += jnp.sum(r32 * u, axis=1, keepdims=True)
        second += jnp.sum(r32 * sums[g, 0:half, :], axis=1, keepdims=True)
    moments[my_rows, :] = jnp.where(lane_h == 0, first, second) / width
    gp_copy(groups).start()

    tile = 256

    def token_tile(j):
        cols = pl.ds(pl.multiple_of(j * tile, tile), tile)
        grad_hidden = nt(gp[:, head : 2 * head], weights[1, cols, :])
        for g in range(2, groups):
            grad_hidden += nt(gp[:, g * head : (g + 1) * head], weights[g, cols, :])
        m = mean_inv[...]
        inv = m[:, 1:2]
        normed = (tok_ref[:, cols].astype(F32) - m[:, 0:1]) * inv
        mo = moments[...]
        grad_normed = grad_hidden * gain_ref[:, cols]
        gt_ref[:, cols] = (
            go_ref[:, cols].astype(F32)
            + inv * (grad_normed - mo[:, 0:1] - normed * mo[:, 1:2])
        ).astype(BF16)

    tiles = local // tile
    for g in (3, 1, 2):
        y_phase(g)
    chain(0)
    own_phase(3)
    gp_arrived(groups)
    for j in range(tiles // 2):
        token_tile(j)
    chain(3)
    chain_end(0)
    own_phase(1)
    for j in range(tiles // 2, tiles):
        token_tile(j)
    chain(1)
    own_phase(2)
    gain_sum = chain_end(3)
    chain(2)
    gain_sum += chain_end(1)
    gain_sum += chain_end(2)
    gain_pad[...] = jnp.zeros_like(gain_pad)
    gain_pad[0:depth, :] = gain_sum / gain_t[mine, :]
    ggain_ref[...] = gain_pad[...].T[0:1, 0:depth]

    gather_sent()
    for k in range(1, 4):
        stat_copy(k).wait_send()
    for g in range(groups):
        core_copy(g).wait_send()
        x_copy(g).wait_send()
    for k in range(groups + 1):
        gp_copy(k).wait_send()
    for g in range(groups):
        for k in range(nz):
            y_copy(g, k).wait_send()
            pl.when(z > k)(lambda: chain_copy(g, 0, k).wait_send())
            pl.when(z < k)(lambda: chain_copy(g, 1, k).wait_send())


def fused(nz, width, tokens, grad_out, gain, qkv_weight, out_weight):
    rows, local = tokens.shape
    head = out_weight.shape[0]
    depth = qkv_weight.shape[0]
    half = rows // 2
    n = 2 * nz
    vmem = pl.BlockSpec(memory_space=pltpu.VMEM)
    hbm = pl.BlockSpec(memory_space=pltpu.HBM)
    dma = pltpu.SemaphoreType.DMA
    exchange = pltpu.VMEM((4, half + 8, head), F32)
    pieces = pltpu.VMEM((nz, depth, 4 * head), BF16)
    return pl.pallas_call(
        functools.partial(kernel, nz, width),
        out_shape=(
            jax.ShapeDtypeStruct((rows, local), BF16),
            jax.ShapeDtypeStruct((depth, 4 * head), F32),
            jax.ShapeDtypeStruct((1, depth), F32),
        ),
        in_specs=[hbm, hbm, vmem, hbm, hbm],
        out_specs=(vmem, vmem, vmem),
        scratch_shapes=[
            pltpu.VMEM((rows, local), BF16),
            pltpu.VMEM((rows, local), BF16),
            pltpu.VMEM((4, local, head), BF16),
            pltpu.VMEM((rows, local), BF16),
            pltpu.VMEM((local, rows), BF16),
            pltpu.VMEM((local, rows), BF16),
            pltpu.VMEM((local, 128), F32),
            pltpu.VMEM((-(-depth // 128) * 128, 128), F32),
            pltpu.VMEM((4, 8, rows), F32),
            pltpu.VMEM((rows, 128), F32),
            exchange,
            exchange,
            exchange,
            exchange,
            exchange,
            pltpu.VMEM((rows, 4 * head), BF16),
            pltpu.VMEM((rows, 128), F32),
            exchange,
            pieces,
            pieces,
            pltpu.VMEM((nz, depth, 4 * head), F32),
            pltpu.VMEM((2, nz, depth, 4 * head), BF16),
            pltpu.VMEM((2, nz, depth, 4 * head), BF16),
            dma((6,)),
            dma((4, 3, nz)),
            dma((4, n)),
            dma((4,)),
            dma((4,)),
            dma((4,)),
            dma((4,)),
            dma((4,)),
            dma((4,)),
            dma((5,)),
            dma((5,)),
            dma((4, nz)),
            dma((4, nz)),
            dma((4, 2, nz)),
            dma((4, 2, nz)),
        ],
        compiler_params=pltpu.CompilerParams(
            collective_id=0, has_side_effects=True, vmem_limit_bytes=52 * 1024 * 1024
        ),
        name="head_backward",
    )(tokens, grad_out, gain.reshape(1, local), qkv_weight, out_weight.T)


def on_device(tokens, grad_out, gain, qkv_weight, out_weight):
    tok_rows, local_width = tokens.shape
    model_width = local_width * lax.axis_size("sec")
    head_size = out_weight.shape[0]
    shards = lax.axis_size("fsdp")
    depth = qkv_weight.shape[0]
    if depth % 64 or tok_rows != 2 * PATCHES or lax.axis_size("sec") != 4 or shards % 2:
        return by_collectives(tokens, grad_out, gain, qkv_weight, out_weight)
    grad_tokens, grads, grad_gain = fused(
        shards // 2, model_width, tokens, grad_out, gain, qkv_weight, out_weight
    )
    return grad_tokens, grads[:, head_size:], grads[:, :head_size].T, grad_gain.reshape(depth)


def by_collectives(tokens, grad_out, gain, qkv_weight, out_weight):
    tok_rows, local_width = tokens.shape
    model_width = local_width * lax.axis_size("sec")
    head_size = out_weight.shape[0]
    images = tok_rows // PATCHES
    tok_float = tokens.astype(jnp.float32)
    row_sums, row_squares = lax.psum(
        (jnp.sum(tok_float, axis=1), jnp.sum(tok_float * tok_float, axis=1)), "sec"
    )
    row_mean = row_sums / model_width
    row_var = row_squares / model_width - row_mean * row_mean
    inv_std = lax.rsqrt(row_var + EPS)
    normed = (tok_float - row_mean[:, None]) * inv_std[:, None]
    hidden = (normed * gain[None, :]).astype(jnp.bfloat16)
    columns = hidden
    partial_value = jnp.dot(
        columns,
        lax.all_gather(qkv_weight, "fsdp", axis=0, tiled=True),
        preferred_element_type=jnp.float32,
    )
    proj = lax.psum(partial_value, "sec").astype(jnp.bfloat16)
    parts = proj.reshape(images, PATCHES, 3, head_size)
    query, key_in, value = (parts[:, :, 0], parts[:, :, 1], parts[:, :, 2])
    scale = 1.0 / head_size**0.5
    scores = jnp.einsum("ipd,iqd->ipq", query, key_in, preferred_element_type=jnp.float32) * scale
    probs = jax.nn.softmax(scores, axis=-1)
    probs_b = probs.astype(jnp.bfloat16)
    attended = jnp.einsum(
        "ipq,iqd->ipd", probs_b, value, preferred_element_type=jnp.float32
    ).astype(jnp.bfloat16)
    attended = attended.reshape(tok_rows, head_size)
    local_outw = lax.dot_general(
        attended, grad_out, (((0,), (0,)), ((), ())), preferred_element_type=jnp.float32
    )
    grad_outw = lax.psum_scatter(local_outw, "fsdp", scatter_dimension=1, tiled=True)
    columns = grad_out
    att_partial = lax.dot_general(
        columns,
        lax.all_gather(out_weight, "fsdp", axis=1, tiled=True),
        (((1,), (1,)), ((), ())),
        preferred_element_type=jnp.float32,
    )
    grad_att = lax.psum(att_partial, "sec").astype(jnp.bfloat16)
    grad_att3 = grad_att.reshape(images, PATCHES, head_size)
    grad_prob = jnp.einsum("ipd,iqd->ipq", grad_att3, value, preferred_element_type=jnp.float32)
    grad_score = (
        probs * (grad_prob - jnp.sum(grad_prob * probs, axis=-1, keepdims=True)) * scale
    ).astype(jnp.bfloat16)
    grad_query = jnp.einsum("ipq,iqd->ipd", grad_score, key_in, preferred_element_type=jnp.float32)
    grad_key = jnp.einsum("ipq,ipd->iqd", grad_score, query, preferred_element_type=jnp.float32)
    grad_value = jnp.einsum("ipq,ipd->iqd", probs_b, grad_att3, preferred_element_type=jnp.float32)
    grad_proj = (
        jnp.stack([grad_query, grad_key, grad_value], axis=2)
        .reshape(tok_rows, 3 * head_size)
        .astype(jnp.bfloat16)
    )
    local_qkv = lax.dot_general(
        hidden, grad_proj, (((0,), (0,)), ((), ())), preferred_element_type=jnp.float32
    )
    grad_hidden = lax.dot_general(
        grad_proj,
        lax.all_gather(qkv_weight, "fsdp", axis=0, tiled=True),
        (((1,), (1,)), ((), ())),
        preferred_element_type=jnp.float32,
    )
    local_gain = jnp.sum(grad_hidden * normed, axis=0)
    grad_normed = grad_hidden * gain[None, :]
    first_sum, second_sum = lax.psum(
        (jnp.sum(grad_normed, axis=1), jnp.sum(grad_normed * normed, axis=1)), "sec"
    )
    first = first_sum / model_width
    second = second_sum / model_width
    grad_tokens = grad_out.astype(jnp.float32) + inv_std[:, None] * (
        grad_normed - first[:, None] - normed * second[:, None]
    )
    grad_qkv, grad_gain = (
        lax.psum_scatter(local_qkv, "fsdp", scatter_dimension=0, tiled=True),
        lax.psum_scatter(local_gain, "fsdp", scatter_dimension=0, tiled=True),
    )
    return (grad_tokens.astype(jnp.bfloat16), grad_qkv, grad_outw, grad_gain)


def solution(mesh):
    placed = (
        P("fsdp", "sec"),
        P("fsdp", "sec"),
        P("sec"),
        P(("sec", "fsdp"), None),
        P(None, ("sec", "fsdp")),
    )
    return jax.shard_map(
        on_device,
        mesh=mesh,
        in_specs=placed,
        out_specs=(
            P("fsdp", "sec"),
            P(("sec", "fsdp"), None),
            P(None, ("sec", "fsdp")),
            P(("sec", "fsdp")),
        ),
        check_vma=False,
    )
```

```python
import functools

import jax
import jax.numpy as jnp
from jax import lax
from jax.experimental import pallas as pl
from jax.experimental.pallas import tpu as pltpu
from jax.sharding import PartitionSpec as P

PATCHES = 256
EPS = 1e-06
MESH = pl.DeviceIdType.MESH
F32 = jnp.float32
BF16 = jnp.bfloat16


def nn(a, b):
    return jnp.dot(a, b, preferred_element_type=F32)


def nt(a, b):
    return lax.dot_general(a, b, (((1,), (1,)), ((), ())), preferred_element_type=F32)


def tn(a, b):
    return lax.dot_general(a, b, (((0,), (0,)), ((), ())), preferred_element_type=F32)


def copy_to(src, dst, send, recv, device):
    return pltpu.make_async_remote_copy(
        src_ref=src,
        dst_ref=dst,
        send_sem=send,
        recv_sem=recv,
        device_id=device,
        device_id_type=MESH,
    )


def kernel(
    nz,
    width,
    tok_hbm,
    go_hbm,
    gain_ref,
    qkv_hbm,
    ow_hbm,
    gt_ref,
    grad_ref,
    ggain_ref,
    tok_ref,
    go_ref,
    weights,
    hidden,
    hidden_t,
    go_t,
    gain_t,
    gain_pad,
    stats,
    mean_inv,
    first_out,
    first_own,
    first_in,
    second_out,
    second_in,
    gp,
    moments,
    sums,
    y_out,
    y_in,
    own,
    chain_out,
    chain_in,
    load_sem,
    gather_send,
    gather_recv,
    stat_send,
    stat_recv,
    core_send,
    core_recv,
    x_send,
    x_recv,
    gp_send,
    gp_recv,
    y_send,
    y_recv,
    chain_send,
    chain_recv,
):
    rows, local = tok_ref.shape
    depth, head = ow_hbm.shape
    groups = weights.shape[0]
    half = rows // 2
    s = lax.axis_index("sec")
    f = lax.axis_index("fsdp")
    z, y = f // 2, f % 2
    c = s % 2
    core = {"sec": s + 1 - 2 * c}
    across = {"sec": (s + 2) % 4}
    other_y = {"fsdp": f + 1 - 2 * y}
    to_left = {"fsdp": f - 2}
    to_right = {"fsdp": f + 2}
    has_left = z > 0
    has_right = z < nz - 1

    barrier = pltpu.get_barrier_semaphore()

    def greet(device):
        pl.semaphore_signal(barrier, inc=1, device_id=device, device_id_type=MESH)

    greet(other_y)
    for k in range(1, 4):
        greet({"sec": (s + k) % 4})
    pl.when(has_left)(lambda: greet(to_left))
    pl.when(has_right)(lambda: greet(to_right))

    mine = pl.ds(pl.multiple_of(f * depth, depth), depth)
    loads = [pltpu.make_async_copy(ow_hbm, weights.at[0, mine, :], load_sem.at[0])]
    for g in range(1, groups):
        part_hbm = qkv_hbm.at[:, pl.ds((g - 1) * head, head)]
        loads.append(pltpu.make_async_copy(part_hbm, weights.at[g, mine, :], load_sem.at[g]))
    loads.append(pltpu.make_async_copy(tok_hbm, tok_ref, load_sem.at[4]))
    loads.append(pltpu.make_async_copy(go_hbm, go_ref, load_sem.at[5]))
    for load in loads:
        load.start()

    peers = 4 + has_left.astype(jnp.int32) + has_right.astype(jnp.int32)
    pl.semaphore_wait(barrier, peers)

    def block(g, shard):
        return weights.at[g, pl.ds(pl.multiple_of(shard * depth, depth), depth), :]

    def gather_copy(g, shard_z, way, device):
        shard = shard_z * 2 + y
        ref = block(g, shard)
        return copy_to(
            ref, ref, gather_send.at[g, way, shard_z], gather_recv.at[g, shard], device
        )

    def go_left(g, shard_z):
        return gather_copy(g, shard_z, 0, to_left)

    def go_right(g, shard_z):
        return gather_copy(g, shard_z, 1, to_right)

    def go_y(g, shard_z):
        return gather_copy(g, shard_z, 2, other_y)

    def arrived(g, shard):
        ref = block(g, shard)
        copy_to(
            ref, ref, gather_send.at[g, 0, 0], gather_recv.at[g, shard], other_y
        ).wait_recv()

    def send_own(g):
        pl.when(has_left)(lambda: go_left(g, z).start())
        pl.when(has_right)(lambda: go_right(g, z).start())
        go_y(g, z).start()

    def forward(g, d):
        @pl.when(z - d >= 0)
        def _():
            arrived(g, (z - d) * 2 + y)
            pl.when(has_right)(lambda: go_right(g, z - d).start())
            go_y(g, z - d).start()

        @pl.when(z + d < nz)
        def _():
            arrived(g, (z + d) * 2 + y)
            pl.when(has_left)(lambda: go_left(g, z + d).start())
            go_y(g, z + d).start()

    turn_order = (1, 2, 3, 0)

    def wave(w):
        for g_at, g in enumerate(turn_order):
            if 1 <= w - g_at < nz:
                forward(g, w - g_at)

    def gathered(g):
        for shard_z in range(nz):
            arrived(g, shard_z * 2 + 1 - y)

    def gather_sent():
        for g in range(groups):
            for shard_z in range(nz):
                pl.when(has_left & (z <= shard_z))(lambda: go_left(g, shard_z).wait_send())
                pl.when(has_right & (z >= shard_z))(lambda: go_right(g, shard_z).wait_send())
                go_y(g, shard_z).wait_send()

    loads[1].wait()
    send_own(1)
    loads[2].wait()
    send_own(2)
    loads[4].wait()

    step = 64
    lane = lax.broadcasted_iota(jnp.int32, (step, 128), 1)

    def row_sums(i, carry):
        r = pl.ds(pl.multiple_of(i * step, step), step)
        t = tok_ref[r, :].astype(F32)
        a = jnp.sum(t, axis=1, keepdims=True)
        b = jnp.sum(t * t, axis=1, keepdims=True)
        mean_inv[r, :] = jnp.where(lane == 0, a, b)
        return carry

    lax.fori_loop(0, rows // step, row_sums, 0)
    stats[s] = mean_inv[...].T[:8, :]

    def stat_copy(k):
        return copy_to(
            stats.at[s], stats.at[s], stat_send.at[k], stat_recv.at[s], {"sec": (s + k) % 4}
        )

    for k in range(1, 4):
        stat_copy(k).start()

    wave(1)
    loads[3].wait()
    send_own(3)
    wave(2)
    loads[0].wait()
    send_own(0)
    wave(3)
    loads[5].wait()

    tstep = 256

    def turn(src, dst):
        for i in range(rows // tstep):

            def body(j, carry):
                cols = pl.ds(pl.multiple_of(j * tstep, tstep), tstep)
                part = src[i * tstep : (i + 1) * tstep, cols].astype(F32)
                dst[cols, i * tstep : (i + 1) * tstep] = part.T.astype(BF16)
                return carry

            lax.fori_loop(0, local // tstep, body, 0)


    gain_row = gain_ref[...]
    g_hi = gain_row.astype(BF16)
    rest = gain_row - g_hi.astype(F32)
    g_mid = rest.astype(BF16)
    g_lo = (rest - g_mid.astype(F32)).astype(BF16)
    row16 = lax.broadcasted_iota(jnp.int32, (16, local), 0)
    gain16 = jnp.where(
        row16 == 0,
        g_hi.astype(F32),
        jnp.where(row16 == 1, g_mid.astype(F32), jnp.where(row16 == 2, g_lo.astype(F32), 0.0)),
    ).astype(BF16)

    my_rows = pl.ds(pl.multiple_of(c * half, half), half)
    their_rows = pl.ds(pl.multiple_of((1 - c) * half, half), half)

    def core_copy(g):
        return copy_to(
            first_out.at[g], first_in.at[g], core_send.at[g], core_recv.at[g], core
        )

    def x_copy(g):
        return copy_to(
            second_out.at[g], second_in.at[g], x_send.at[g], x_recv.at[g], across
        )

    def project(g, left):
        w = weights[g]
        u = jnp.sum(nn(gain16, w), axis=0, keepdims=True)
        u = jnp.broadcast_to(u, (8, head))
        first_out[g, half : half + 8, :] = u
        first_out[g, 0:half, :] = nn(left[their_rows, :], w)
        core_copy(g).start()
        first_own[g, half : half + 8, :] = u
        first_own[g, 0:half, :] = nn(left[my_rows, :], w)

    def across_start(g):
        core_copy(g).wait_recv()
        second_out[g] = first_own[g] + first_in[g]
        x_copy(g).start()


    for k in range(1, 4):
        sender = (s + k) % 4
        copy_to(
            stats.at[sender], stats.at[sender], stat_send.at[k], stat_recv.at[sender], core
        ).wait_recv()
    total = stats[0] + stats[1] + stats[2] + stats[3]
    row_mean = total[0:1, :] / width
    row_var = total[1:2, :] / width - row_mean * row_mean
    inv_std = lax.rsqrt(row_var + EPS)
    sub = lax.broadcasted_iota(jnp.int32, (128, rows), 0)
    mean_inv[...] = jnp.where(sub == 0, row_mean, inv_std).T

    def norm(i, carry):
        r = pl.ds(pl.multiple_of(i * step, step), step)
        t = tok_ref[r, :].astype(F32)
        m = mean_inv[r, :]
        normed = (t - m[:, 0:1]) * m[:, 1:2]
        hidden[r, :] = (normed * gain_ref[...]).astype(BF16)
        return carry

    lax.fori_loop(0, rows // step, norm, 0)

    wave(4)
    gathered(1)
    project(1, hidden)
    wave(5)
    across_start(1)
    for w in range(6, nz + len(turn_order) - 1):
        wave(w)
    gathered(2)
    project(2, hidden)
    turn(go_ref, go_t)
    across_start(2)
    gathered(3)
    project(3, hidden)
    turn(hidden, hidden_t)
    across_start(3)
    gain_t[...] = jnp.broadcast_to(gain_ref[...], (128, local)).T
    gathered(0)
    project(0, go_ref)

    def finish(g):
        x_copy(g).wait_recv()
        sums[g] = second_out[g] + second_in[g]
        return sums[g, 0:half, :].astype(BF16)

    scale = 1.0 / head**0.5
    query = finish(1)
    key = finish(2)
    scores = nt(query, key) * scale
    e = jnp.exp(scores - jnp.max(scores, axis=-1, keepdims=True))
    probs = e / jnp.sum(e, axis=-1, keepdims=True)
    probs_b = probs.astype(BF16)
    across_start(0)

    def gp_piece(k, r):
        return moments.at[r, :] if k == groups else gp.at[r, pl.ds(k * head, head)]

    def gp_copy(k):
        ref = gp_piece(k, my_rows)
        return copy_to(ref, ref, gp_send.at[k], gp_recv.at[k], core)

    def gp_arrived(k):
        ref = gp_piece(k, their_rows)
        copy_to(ref, ref, gp_send.at[k], gp_recv.at[k], core).wait_recv()

    def gp_put(k, result):
        rounded = result.astype(BF16)
        gp[my_rows, k * head : (k + 1) * head] = rounded
        gp_copy(k).start()
        return rounded

    value = finish(3)
    gp_put(0, nn(probs_b, value))

    def span(g):
        return slice(g * head, (g + 1) * head)

    def cols_of(g):
        return pl.ds(g * head, head)

    near = (z < nz // 2).astype(jnp.int32)

    def far_end(way, k):
        return way * (nz - 1 - k) + (1 - way) * k

    def part(g, shard):
        r = pl.ds(pl.multiple_of(shard * depth, depth), depth)
        return nn((go_t if g == 0 else hidden_t)[r, :], gp[:, span(g)])

    def y_copy(g, shard_z):
        return copy_to(
            y_out.at[shard_z, :, cols_of(g)],
            y_in.at[shard_z, :, cols_of(g)],
            y_send.at[g, shard_z],
            y_recv.at[g, shard_z],
            other_y,
        )

    def y_phase(g):
        gp_arrived(g)
        for k in range(nz):
            shard_z = far_end(near, k)
            y_out[shard_z, :, span(g)] = part(g, shard_z * 2 + 1 - y).astype(BF16)
            y_copy(g, shard_z).start()

    def own_phase(g):
        for k in range(nz):
            own[k, :, span(g)] = part(g, k * 2 + y)

    def chain_copy(g, way, dest):
        return copy_to(
            chain_out.at[way, dest, :, cols_of(g)],
            chain_in.at[way, dest, :, cols_of(g)],
            chain_send.at[g, way, dest],
            chain_recv.at[g, way, dest],
            {"fsdp": f + 4 * way - 2},
        )

    def chain(g, leg):
        way = near if leg == 0 else 1 - near
        follows = ((way == 1) & has_left) | ((way == 0) & has_right)
        for k in range(nz - 1):
            dest = far_end(way, k)
            passes = ((way == 1) & (dest > z)) | ((way == 0) & (dest < z))

            @pl.when(passes)
            def _():
                y_copy(g, dest).wait_recv()
                here = own[dest, :, span(g)] + y_in[dest, :, span(g)].astype(F32)

                @pl.when(follows)
                def _():
                    chain_copy(g, way, dest).wait_recv()
                    chain_out[way, dest, :, span(g)] = (
                        here + chain_in[way, dest, :, span(g)].astype(F32)
                    ).astype(BF16)

                @pl.when(jnp.logical_not(follows))
                def _():
                    chain_out[way, dest, :, span(g)] = here.astype(BF16)

                chain_copy(g, way, dest).start()

    def chain_end(g):
        y_copy(g, z).wait_recv()
        grad_ref[:, span(g)] = own[z, :, span(g)] + y_in[z, :, span(g)].astype(F32)

        @pl.when(has_left)
        def _():
            chain_copy(g, 1, z).wait_recv()
            grad_ref[:, span(g)] += chain_in[1, z, :, span(g)].astype(F32)

        @pl.when(has_right)
        def _():
            chain_copy(g, 0, z).wait_recv()
            grad_ref[:, span(g)] += chain_in[0, z, :, span(g)].astype(F32)

        if g == 0:
            return 0.0
        held = weights[g, mine, :].astype(F32)
        return jnp.sum(held * grad_ref[:, span(g)], axis=1, keepdims=True)

    y_phase(0)
    own_phase(0)

    grad_att = finish(0)
    grad_value = gp_put(3, tn(probs_b, grad_att))
    grad_prob = nt(grad_att, value)
    grad_score = (
        probs * (grad_prob - jnp.sum(grad_prob * probs, axis=-1, keepdims=True)) * scale
    ).astype(BF16)
    grad_query = gp_put(1, nn(grad_score, key))
    grad_key = gp_put(2, tn(grad_score, query))
    lane_h = lax.broadcasted_iota(jnp.int32, (half, 128), 1)
    first = jnp.zeros((half, 1), F32)
    second = jnp.zeros((half, 1), F32)
    for g, grad in ((1, grad_query), (2, grad_key), (3, grad_value)):
        r32 = grad.astype(F32)
        u = sums[g, half : half + 1, :]
        first += jnp.sum(r32 * u, axis=1, keepdims=True)
        second += jnp.sum(r32 * sums[g, 0:half, :], axis=1, keepdims=True)
    moments[my_rows, :] = jnp.where(lane_h == 0, first, second) / width
    gp_copy(groups).start()

    tile = 256

    def token_tile(j):
        cols = pl.ds(pl.multiple_of(j * tile, tile), tile)
        grad_hidden = nt(gp[:, head : 2 * head], weights[1, cols, :])
        for g in range(2, groups):
            grad_hidden += nt(gp[:, g * head : (g + 1) * head], weights[g, cols, :])
        m = mean_inv[...]
        inv = m[:, 1:2]
        normed = (tok_ref[:, cols].astype(F32) - m[:, 0:1]) * inv
        mo = moments[...]
        grad_normed = grad_hidden * gain_ref[:, cols]
        gt_ref[:, cols] = (
            go_ref[:, cols].astype(F32)
            + inv * (grad_normed - mo[:, 0:1] - normed * mo[:, 1:2])
        ).astype(BF16)

    tiles = local // tile
    for g in (3, 1, 2):
        y_phase(g)
    cuts = [tiles * k // 3 for k in range(4)]

    def some_tiles(k):
        for j in range(cuts[k], cuts[k + 1]):
            token_tile(j)

    chain(0, 0)
    own_phase(3)
    chain(0, 1)
    gp_arrived(groups)
    some_tiles(0)
    chain(3, 0)
    own_phase(1)
    chain_end(0)
    some_tiles(1)
    chain(1, 0)
    chain(3, 1)
    own_phase(2)
    gain_sum = chain_end(3)
    chain(2, 0)
    chain(1, 1)
    some_tiles(2)
    chain(2, 1)
    gain_sum += chain_end(1)
    gain_sum += chain_end(2)
    gain_pad[...] = jnp.zeros_like(gain_pad)
    gain_pad[0:depth, :] = gain_sum / gain_t[mine, :]
    ggain_ref[...] = gain_pad[...].T[0:1, 0:depth]

    gather_sent()
    for k in range(1, 4):
        stat_copy(k).wait_send()
    for g in range(groups):
        core_copy(g).wait_send()
        x_copy(g).wait_send()
    for k in range(groups + 1):
        gp_copy(k).wait_send()
    for g in range(groups):
        for k in range(nz):
            y_copy(g, k).wait_send()
            pl.when(z > k)(lambda: chain_copy(g, 0, k).wait_send())
            pl.when(z < k)(lambda: chain_copy(g, 1, k).wait_send())


def fused(nz, width, tokens, grad_out, gain, qkv_weight, out_weight):
    rows, local = tokens.shape
    head = out_weight.shape[0]
    depth = qkv_weight.shape[0]
    half = rows // 2
    n = 2 * nz
    vmem = pl.BlockSpec(memory_space=pltpu.VMEM)
    hbm = pl.BlockSpec(memory_space=pltpu.HBM)
    dma = pltpu.SemaphoreType.DMA
    exchange = pltpu.VMEM((4, half + 8, head), F32)
    pieces = pltpu.VMEM((nz, depth, 4 * head), BF16)
    return pl.pallas_call(
        functools.partial(kernel, nz, width),
        out_shape=(
            jax.ShapeDtypeStruct((rows, local), BF16),
            jax.ShapeDtypeStruct((depth, 4 * head), F32),
            jax.ShapeDtypeStruct((1, depth), F32),
        ),
        in_specs=[hbm, hbm, vmem, hbm, hbm],
        out_specs=(vmem, vmem, vmem),
        scratch_shapes=[
            pltpu.VMEM((rows, local), BF16),
            pltpu.VMEM((rows, local), BF16),
            pltpu.VMEM((4, local, head), BF16),
            pltpu.VMEM((rows, local), BF16),
            pltpu.VMEM((local, rows), BF16),
            pltpu.VMEM((local, rows), BF16),
            pltpu.VMEM((local, 128), F32),
            pltpu.VMEM((-(-depth // 128) * 128, 128), F32),
            pltpu.VMEM((4, 8, rows), F32),
            pltpu.VMEM((rows, 128), F32),
            exchange,
            exchange,
            exchange,
            exchange,
            exchange,
            pltpu.VMEM((rows, 4 * head), BF16),
            pltpu.VMEM((rows, 128), F32),
            exchange,
            pieces,
            pieces,
            pltpu.VMEM((nz, depth, 4 * head), F32),
            pltpu.VMEM((2, nz, depth, 4 * head), BF16),
            pltpu.VMEM((2, nz, depth, 4 * head), BF16),
            dma((6,)),
            dma((4, 3, nz)),
            dma((4, n)),
            dma((4,)),
            dma((4,)),
            dma((4,)),
            dma((4,)),
            dma((4,)),
            dma((4,)),
            dma((5,)),
            dma((5,)),
            dma((4, nz)),
            dma((4, nz)),
            dma((4, 2, nz)),
            dma((4, 2, nz)),
        ],
        compiler_params=pltpu.CompilerParams(
            collective_id=0, has_side_effects=True, vmem_limit_bytes=50 * 1024 * 1024
        ),
        name="head_backward",
    )(tokens, grad_out, gain.reshape(1, local), qkv_weight, out_weight.T)


def on_device(tokens, grad_out, gain, qkv_weight, out_weight):
    tok_rows, local_width = tokens.shape
    model_width = local_width * lax.axis_size("sec")
    head_size = out_weight.shape[0]
    shards = lax.axis_size("fsdp")
    depth = qkv_weight.shape[0]
    if depth % 64 or tok_rows != 2 * PATCHES or lax.axis_size("sec") != 4 or shards % 2:
        return by_collectives(tokens, grad_out, gain, qkv_weight, out_weight)
    grad_tokens, grads, grad_gain = fused(
        shards // 2, model_width, tokens, grad_out, gain, qkv_weight, out_weight
    )
    return grad_tokens, grads[:, head_size:], grads[:, :head_size].T, grad_gain.reshape(depth)


def by_collectives(tokens, grad_out, gain, qkv_weight, out_weight):
    tok_rows, local_width = tokens.shape
    model_width = local_width * lax.axis_size("sec")
    head_size = out_weight.shape[0]
    images = tok_rows // PATCHES
    tok_float = tokens.astype(jnp.float32)
    row_sums, row_squares = lax.psum(
        (jnp.sum(tok_float, axis=1), jnp.sum(tok_float * tok_float, axis=1)), "sec"
    )
    row_mean = row_sums / model_width
    row_var = row_squares / model_width - row_mean * row_mean
    inv_std = lax.rsqrt(row_var + EPS)
    normed = (tok_float - row_mean[:, None]) * inv_std[:, None]
    hidden = (normed * gain[None, :]).astype(jnp.bfloat16)
    columns = hidden
    partial_value = jnp.dot(
        columns,
        lax.all_gather(qkv_weight, "fsdp", axis=0, tiled=True),
        preferred_element_type=jnp.float32,
    )
    proj = lax.psum(partial_value, "sec").astype(jnp.bfloat16)
    parts = proj.reshape(images, PATCHES, 3, head_size)
    query, key_in, value = (parts[:, :, 0], parts[:, :, 1], parts[:, :, 2])
    scale = 1.0 / head_size**0.5
    scores = jnp.einsum("ipd,iqd->ipq", query, key_in, preferred_element_type=jnp.float32) * scale
    probs = jax.nn.softmax(scores, axis=-1)
    probs_b = probs.astype(jnp.bfloat16)
    attended = jnp.einsum(
        "ipq,iqd->ipd", probs_b, value, preferred_element_type=jnp.float32
    ).astype(jnp.bfloat16)
    attended = attended.reshape(tok_rows, head_size)
    local_outw = lax.dot_general(
        attended, grad_out, (((0,), (0,)), ((), ())), preferred_element_type=jnp.float32
    )
    grad_outw = lax.psum_scatter(local_outw, "fsdp", scatter_dimension=1, tiled=True)
    columns = grad_out
    att_partial = lax.dot_general(
        columns,
        lax.all_gather(out_weight, "fsdp", axis=1, tiled=True),
        (((1,), (1,)), ((), ())),
        preferred_element_type=jnp.float32,
    )
    grad_att = lax.psum(att_partial, "sec").astype(jnp.bfloat16)
    grad_att3 = grad_att.reshape(images, PATCHES, head_size)
    grad_prob = jnp.einsum("ipd,iqd->ipq", grad_att3, value, preferred_element_type=jnp.float32)
    grad_score = (
        probs * (grad_prob - jnp.sum(grad_prob * probs, axis=-1, keepdims=True)) * scale
    ).astype(jnp.bfloat16)
    grad_query = jnp.einsum("ipq,iqd->ipd", grad_score, key_in, preferred_element_type=jnp.float32)
    grad_key = jnp.einsum("ipq,ipd->iqd", grad_score, query, preferred_element_type=jnp.float32)
    grad_value = jnp.einsum("ipq,ipd->iqd", probs_b, grad_att3, preferred_element_type=jnp.float32)
    grad_proj = (
        jnp.stack([grad_query, grad_key, grad_value], axis=2)
        .reshape(tok_rows, 3 * head_size)
        .astype(jnp.bfloat16)
    )
    local_qkv = lax.dot_general(
        hidden, grad_proj, (((0,), (0,)), ((), ())), preferred_element_type=jnp.float32
    )
    grad_hidden = lax.dot_general(
        grad_proj,
        lax.all_gather(qkv_weight, "fsdp", axis=0, tiled=True),
        (((1,), (1,)), ((), ())),
        preferred_element_type=jnp.float32,
    )
    local_gain = jnp.sum(grad_hidden * normed, axis=0)
    grad_normed = grad_hidden * gain[None, :]
    first_sum, second_sum = lax.psum(
        (jnp.sum(grad_normed, axis=1), jnp.sum(grad_normed * normed, axis=1)), "sec"
    )
    first = first_sum / model_width
    second = second_sum / model_width
    grad_tokens = grad_out.astype(jnp.float32) + inv_std[:, None] * (
        grad_normed - first[:, None] - normed * second[:, None]
    )
    grad_qkv, grad_gain = (
        lax.psum_scatter(local_qkv, "fsdp", scatter_dimension=0, tiled=True),
        lax.psum_scatter(local_gain, "fsdp", scatter_dimension=0, tiled=True),
    )
    return (grad_tokens.astype(jnp.bfloat16), grad_qkv, grad_outw, grad_gain)


def solution(mesh):
    placed = (
        P("fsdp", "sec"),
        P("fsdp", "sec"),
        P("sec"),
        P(("sec", "fsdp"), None),
        P(None, ("sec", "fsdp")),
    )
    return jax.shard_map(
        on_device,
        mesh=mesh,
        in_specs=placed,
        out_specs=(
            P("fsdp", "sec"),
            P(("sec", "fsdp"), None),
            P(None, ("sec", "fsdp")),
            P(("sec", "fsdp")),
        ),
        check_vma=False,
    )
```

```python
import functools

import jax
import jax.numpy as jnp
from jax import lax
from jax.experimental import pallas as pl
from jax.experimental.pallas import tpu as pltpu
from jax.sharding import PartitionSpec as P

PATCHES = 256
EPS = 1e-06
MESH = pl.DeviceIdType.MESH
F32 = jnp.float32
BF16 = jnp.bfloat16


def nn(a, b):
    return jnp.dot(a, b, preferred_element_type=F32)


def nt(a, b):
    return lax.dot_general(a, b, (((1,), (1,)), ((), ())), preferred_element_type=F32)


def tn(a, b):
    return lax.dot_general(a, b, (((0,), (0,)), ((), ())), preferred_element_type=F32)


def copy_to(src, dst, send, recv, device):
    return pltpu.make_async_remote_copy(
        src_ref=src,
        dst_ref=dst,
        send_sem=send,
        recv_sem=recv,
        device_id=device,
        device_id_type=MESH,
    )


def kernel(
    nz,
    width,
    tok_hbm,
    go_hbm,
    gain_ref,
    qkv_hbm,
    ow_hbm,
    gt_ref,
    grad_ref,
    ggain_ref,
    tok_ref,
    go_ref,
    weights,
    hidden,
    hidden_t,
    go_t,
    gain_t,
    gain_pad,
    stats,
    mean_inv,
    first_out,
    first_own,
    first_in,
    second_out,
    second_in,
    att_out,
    att_in,
    gp,
    moments,
    sums,
    y_out,
    y_in,
    own,
    chain_out,
    chain_in,
    load_sem,
    gather_send,
    gather_recv,
    stat_send,
    stat_recv,
    core_send,
    core_recv,
    x_send,
    x_recv,
    gp_send,
    gp_recv,
    y_send,
    y_recv,
    chain_send,
    chain_recv,
):
    rows, local = tok_ref.shape
    depth, head = ow_hbm.shape
    groups = weights.shape[0]
    half = rows // 2
    s = lax.axis_index("sec")
    f = lax.axis_index("fsdp")
    z, y = f // 2, f % 2
    c = s % 2
    core = {"sec": s + 1 - 2 * c}
    across = {"sec": (s + 2) % 4}
    other_y = {"fsdp": f + 1 - 2 * y}
    to_left = {"fsdp": f - 2}
    to_right = {"fsdp": f + 2}
    has_left = z > 0
    has_right = z < nz - 1

    barrier = pltpu.get_barrier_semaphore()

    def greet(device):
        pl.semaphore_signal(barrier, inc=1, device_id=device, device_id_type=MESH)

    greet(other_y)
    for k in range(1, 4):
        greet({"sec": (s + k) % 4})
    pl.when(has_left)(lambda: greet(to_left))
    pl.when(has_right)(lambda: greet(to_right))

    mine = pl.ds(pl.multiple_of(f * depth, depth), depth)
    loads = [pltpu.make_async_copy(ow_hbm, weights.at[0, mine, :], load_sem.at[0])]
    for g in range(1, groups):
        part_hbm = qkv_hbm.at[:, pl.ds((g - 1) * head, head)]
        loads.append(pltpu.make_async_copy(part_hbm, weights.at[g, mine, :], load_sem.at[g]))
    loads.append(pltpu.make_async_copy(tok_hbm, tok_ref, load_sem.at[4]))
    loads.append(pltpu.make_async_copy(go_hbm, go_ref, load_sem.at[5]))
    for load in loads:
        load.start()

    peers = 4 + has_left.astype(jnp.int32) + has_right.astype(jnp.int32)
    pl.semaphore_wait(barrier, peers)

    def block(g, shard):
        return weights.at[g, pl.ds(pl.multiple_of(shard * depth, depth), depth), :]

    def gather_copy(g, shard_z, way, device):
        shard = shard_z * 2 + y
        ref = block(g, shard)
        return copy_to(
            ref, ref, gather_send.at[g, way, shard_z], gather_recv.at[g, shard], device
        )

    def go_left(g, shard_z):
        return gather_copy(g, shard_z, 0, to_left)

    def go_right(g, shard_z):
        return gather_copy(g, shard_z, 1, to_right)

    def go_y(g, shard_z):
        return gather_copy(g, shard_z, 2, other_y)

    def arrived(g, shard):
        ref = block(g, shard)
        copy_to(
            ref, ref, gather_send.at[g, 0, 0], gather_recv.at[g, shard], other_y
        ).wait_recv()

    def send_own(g):
        pl.when(has_left)(lambda: go_left(g, z).start())
        pl.when(has_right)(lambda: go_right(g, z).start())
        go_y(g, z).start()

    def forward(g, d):
        @pl.when(z - d >= 0)
        def _():
            arrived(g, (z - d) * 2 + y)
            pl.when(has_right)(lambda: go_right(g, z - d).start())
            go_y(g, z - d).start()

        @pl.when(z + d < nz)
        def _():
            arrived(g, (z + d) * 2 + y)
            pl.when(has_left)(lambda: go_left(g, z + d).start())
            go_y(g, z + d).start()

    turn_order = (1, 2, 3, 0)

    def wave(w):
        for g_at, g in enumerate(turn_order):
            if 1 <= w - g_at < nz:
                forward(g, w - g_at)

    def gathered(g):
        for shard_z in range(nz):
            arrived(g, shard_z * 2 + 1 - y)

    def gather_sent():
        for g in range(groups):
            for shard_z in range(nz):
                pl.when(has_left & (z <= shard_z))(lambda: go_left(g, shard_z).wait_send())
                pl.when(has_right & (z >= shard_z))(lambda: go_right(g, shard_z).wait_send())
                go_y(g, shard_z).wait_send()

    loads[1].wait()
    send_own(1)
    loads[2].wait()
    send_own(2)
    loads[4].wait()

    step = 64
    lane = lax.broadcasted_iota(jnp.int32, (step, 128), 1)

    def row_sums(i, carry):
        r = pl.ds(pl.multiple_of(i * step, step), step)
        t = tok_ref[r, :].astype(F32)
        a = jnp.sum(t, axis=1, keepdims=True)
        b = jnp.sum(t * t, axis=1, keepdims=True)
        mean_inv[r, :] = jnp.where(lane == 0, a, b)
        return carry

    lax.fori_loop(0, rows // step, row_sums, 0)
    stats[s] = mean_inv[...].T[:8, :]

    def stat_copy(k):
        return copy_to(
            stats.at[s], stats.at[s], stat_send.at[k], stat_recv.at[s], {"sec": (s + k) % 4}
        )

    for k in range(1, 4):
        stat_copy(k).start()

    wave(1)
    loads[3].wait()
    send_own(3)
    wave(2)
    loads[0].wait()
    send_own(0)
    wave(3)
    loads[5].wait()

    tstep = 256

    def turn(src, dst):
        for i in range(rows // tstep):

            def body(j, carry):
                cols = pl.ds(pl.multiple_of(j * tstep, tstep), tstep)
                part = src[i * tstep : (i + 1) * tstep, cols].astype(F32)
                dst[cols, i * tstep : (i + 1) * tstep] = part.T.astype(BF16)
                return carry

            lax.fori_loop(0, local // tstep, body, 0)


    gain_row = gain_ref[...]
    g_hi = gain_row.astype(BF16)
    rest = gain_row - g_hi.astype(F32)
    g_mid = rest.astype(BF16)
    g_lo = (rest - g_mid.astype(F32)).astype(BF16)
    row16 = lax.broadcasted_iota(jnp.int32, (16, local), 0)
    gain16 = jnp.where(
        row16 == 0,
        g_hi.astype(F32),
        jnp.where(row16 == 1, g_mid.astype(F32), jnp.where(row16 == 2, g_lo.astype(F32), 0.0)),
    ).astype(BF16)

    my_rows = pl.ds(pl.multiple_of(c * half, half), half)
    their_rows = pl.ds(pl.multiple_of((1 - c) * half, half), half)

    def core_copy(g):
        return copy_to(
            first_out.at[g], first_in.at[g], core_send.at[g], core_recv.at[g], core
        )

    def x_copy(g):
        src, dst = (att_out, att_in) if g == 0 else (second_out.at[g], second_in.at[g])
        return copy_to(src, dst, x_send.at[g], x_recv.at[g], across)

    def project(g, left):
        w = weights[g]
        u = jnp.sum(nn(gain16, w), axis=0, keepdims=True)
        u = jnp.broadcast_to(u, (8, head))
        first_out[g, half : half + 8, :] = u
        first_out[g, 0:half, :] = nn(left[their_rows, :], w)
        core_copy(g).start()
        first_own[g, half : half + 8, :] = u
        first_own[g, 0:half, :] = nn(left[my_rows, :], w)

    def across_start(g):
        core_copy(g).wait_recv()
        if g == 0:
            att_out[...] = (first_own[g, 0:half, :] + first_in[g, 0:half, :]).astype(BF16)
        else:
            second_out[g] = first_own[g] + first_in[g]
        x_copy(g).start()


    for k in range(1, 4):
        sender = (s + k) % 4
        copy_to(
            stats.at[sender], stats.at[sender], stat_send.at[k], stat_recv.at[sender], core
        ).wait_recv()
    total = stats[0] + stats[1] + stats[2] + stats[3]
    row_mean = total[0:1, :] / width
    row_var = total[1:2, :] / width - row_mean * row_mean
    inv_std = lax.rsqrt(row_var + EPS)
    sub = lax.broadcasted_iota(jnp.int32, (128, rows), 0)
    mean_inv[...] = jnp.where(sub == 0, row_mean, inv_std).T

    def norm(i, carry):
        r = pl.ds(pl.multiple_of(i * step, step), step)
        t = tok_ref[r, :].astype(F32)
        m = mean_inv[r, :]
        normed = (t - m[:, 0:1]) * m[:, 1:2]
        hidden[r, :] = (normed * gain_ref[...]).astype(BF16)
        return carry

    lax.fori_loop(0, rows // step, norm, 0)

    wave(4)
    gathered(1)
    project(1, hidden)
    wave(5)
    across_start(1)
    for w in range(6, nz + len(turn_order) - 1):
        wave(w)
    gathered(2)
    project(2, hidden)
    turn(go_ref, go_t)
    across_start(2)
    gathered(3)
    project(3, hidden)
    turn(hidden, hidden_t)
    across_start(3)
    gain_t[...] = jnp.broadcast_to(gain_ref[...], (128, local)).T
    gathered(0)
    project(0, go_ref)

    def finish(g):
        x_copy(g).wait_recv()
        if g == 0:
            return (att_out[...].astype(F32) + att_in[...].astype(F32)).astype(BF16)
        sums[g] = second_out[g] + second_in[g]
        return sums[g, 0:half, :].astype(BF16)

    scale = 1.0 / head**0.5
    query = finish(1)
    key = finish(2)
    scores = nt(query, key) * scale
    e = jnp.exp(scores - jnp.max(scores, axis=-1, keepdims=True))
    probs = e / jnp.sum(e, axis=-1, keepdims=True)
    probs_b = probs.astype(BF16)
    across_start(0)

    def gp_piece(k, r):
        return moments.at[r, :] if k == groups else gp.at[k, r, :]

    def gp_copy(k):
        ref = gp_piece(k, my_rows)
        return copy_to(ref, ref, gp_send.at[k], gp_recv.at[k], core)

    def gp_arrived(k):
        ref = gp_piece(k, their_rows)
        copy_to(ref, ref, gp_send.at[k], gp_recv.at[k], core).wait_recv()

    def gp_put(k, result):
        rounded = result.astype(BF16)
        gp[k, my_rows, :] = rounded
        gp_copy(k).start()
        return rounded

    value = finish(3)
    gp_put(0, nn(probs_b, value))

    def span(g):
        return slice(g * head, (g + 1) * head)

    near = (z < nz // 2).astype(jnp.int32)

    def far_end(way, k):
        return way * (nz - 1 - k) + (1 - way) * k

    def part(g, shard):
        r = pl.ds(pl.multiple_of(shard * depth, depth), depth)
        return nn((go_t if g == 0 else hidden_t)[r, :], gp[g])

    def y_copy(g, shard_z):
        return copy_to(
            y_out.at[g, shard_z],
            y_in.at[g, shard_z],
            y_send.at[g, shard_z],
            y_recv.at[g, shard_z],
            other_y,
        )

    def y_phase(g):
        gp_arrived(g)
        for k in range(nz):
            shard_z = far_end(near, k)
            y_out[g, shard_z] = part(g, shard_z * 2 + 1 - y).astype(BF16)
            y_copy(g, shard_z).start()

    def own_phase(g):
        for k in range(nz):
            own[g, k] = part(g, k * 2 + y)

    def chain_copy(g, way, dest):
        return copy_to(
            chain_out.at[g, way, dest],
            chain_in.at[g, way, dest],
            chain_send.at[g, way, dest],
            chain_recv.at[g, way, dest],
            {"fsdp": f + 4 * way - 2},
        )

    def chain(g, leg):
        way = near if leg == 0 else 1 - near
        follows = ((way == 1) & has_left) | ((way == 0) & has_right)
        for k in range(nz - 1):
            dest = far_end(way, k)
            passes = ((way == 1) & (dest > z)) | ((way == 0) & (dest < z))

            @pl.when(passes)
            def _():
                y_copy(g, dest).wait_recv()
                here = own[g, dest] + y_in[g, dest].astype(F32)

                @pl.when(follows)
                def _():
                    chain_copy(g, way, dest).wait_recv()
                    chain_out[g, way, dest] = (
                        here + chain_in[g, way, dest].astype(F32)
                    ).astype(BF16)

                @pl.when(jnp.logical_not(follows))
                def _():
                    chain_out[g, way, dest] = here.astype(BF16)

                chain_copy(g, way, dest).start()

    def chain_end(g):
        y_copy(g, z).wait_recv()
        grad_ref[:, span(g)] = own[g, z] + y_in[g, z].astype(F32)

        @pl.when(has_left)
        def _():
            chain_copy(g, 1, z).wait_recv()
            grad_ref[:, span(g)] += chain_in[g, 1, z].astype(F32)

        @pl.when(has_right)
        def _():
            chain_copy(g, 0, z).wait_recv()
            grad_ref[:, span(g)] += chain_in[g, 0, z].astype(F32)

        if g == 0:
            return 0.0
        held = weights[g, mine, :].astype(F32)
        return jnp.sum(held * grad_ref[:, span(g)], axis=1, keepdims=True)

    y_phase(0)

    grad_att = finish(0)
    grad_value = gp_put(3, tn(probs_b, grad_att))
    grad_prob = nt(grad_att, value)
    grad_score = (
        probs * (grad_prob - jnp.sum(grad_prob * probs, axis=-1, keepdims=True)) * scale
    ).astype(BF16)
    grad_query = gp_put(1, nn(grad_score, key))
    grad_key = gp_put(2, tn(grad_score, query))
    lane_h = lax.broadcasted_iota(jnp.int32, (half, 128), 1)
    first = jnp.zeros((half, 1), F32)
    second = jnp.zeros((half, 1), F32)
    for g, grad in ((1, grad_query), (2, grad_key), (3, grad_value)):
        r32 = grad.astype(F32)
        u = sums[g, half : half + 1, :]
        first += jnp.sum(r32 * u, axis=1, keepdims=True)
        second += jnp.sum(r32 * sums[g, 0:half, :], axis=1, keepdims=True)
    moments[my_rows, :] = jnp.where(lane_h == 0, first, second) / width
    gp_copy(groups).start()

    tile = 256

    def token_tile(j):
        cols = pl.ds(pl.multiple_of(j * tile, tile), tile)
        grad_hidden = nt(gp[1], weights[1, cols, :])
        for g in range(2, groups):
            grad_hidden += nt(gp[g], weights[g, cols, :])
        m = mean_inv[...]
        inv = m[:, 1:2]
        normed = (tok_ref[:, cols].astype(F32) - m[:, 0:1]) * inv
        mo = moments[...]
        grad_normed = grad_hidden * gain_ref[:, cols]
        gt_ref[:, cols] = (
            go_ref[:, cols].astype(F32)
            + inv * (grad_normed - mo[:, 0:1] - normed * mo[:, 1:2])
        ).astype(BF16)

    tiles = local // tile
    for g in (3, 1, 2):
        y_phase(g)
    cuts = [tiles * k // 3 for k in range(4)]

    def some_tiles(k):
        for j in range(cuts[k], cuts[k + 1]):
            token_tile(j)

    own_phase(0)
    chain(0, 0)
    own_phase(3)
    chain(0, 1)
    gp_arrived(groups)
    some_tiles(0)
    chain(3, 0)
    own_phase(1)
    chain_end(0)
    some_tiles(1)
    chain(1, 0)
    chain(3, 1)
    own_phase(2)
    gain_sum = chain_end(3)
    chain(2, 0)
    chain(1, 1)
    some_tiles(2)
    chain(2, 1)
    gain_sum += chain_end(1)
    gain_sum += chain_end(2)
    gain_pad[...] = jnp.zeros_like(gain_pad)
    gain_pad[0:depth, :] = gain_sum / gain_t[mine, :]
    ggain_ref[...] = gain_pad[...].T[0:1, 0:depth]

    gather_sent()
    for k in range(1, 4):
        stat_copy(k).wait_send()
    for g in range(groups):
        core_copy(g).wait_send()
        x_copy(g).wait_send()
    for k in range(groups + 1):
        gp_copy(k).wait_send()
    for g in range(groups):
        for k in range(nz):
            y_copy(g, k).wait_send()
            pl.when(z > k)(lambda: chain_copy(g, 0, k).wait_send())
            pl.when(z < k)(lambda: chain_copy(g, 1, k).wait_send())


def fused(nz, width, tokens, grad_out, gain, qkv_weight, out_weight):
    rows, local = tokens.shape
    head = out_weight.shape[0]
    depth = qkv_weight.shape[0]
    half = rows // 2
    n = 2 * nz
    vmem = pl.BlockSpec(memory_space=pltpu.VMEM)
    hbm = pl.BlockSpec(memory_space=pltpu.HBM)
    dma = pltpu.SemaphoreType.DMA
    exchange = pltpu.VMEM((4, half + 8, head), F32)
    pieces = pltpu.VMEM((4, nz, depth, head), BF16)
    return pl.pallas_call(
        functools.partial(kernel, nz, width),
        out_shape=(
            jax.ShapeDtypeStruct((rows, local), BF16),
            jax.ShapeDtypeStruct((depth, 4 * head), F32),
            jax.ShapeDtypeStruct((1, depth), F32),
        ),
        in_specs=[hbm, hbm, vmem, hbm, hbm],
        out_specs=(vmem, vmem, vmem),
        scratch_shapes=[
            pltpu.VMEM((rows, local), BF16),
            pltpu.VMEM((rows, local), BF16),
            pltpu.VMEM((4, local, head), BF16),
            pltpu.VMEM((rows, local), BF16),
            pltpu.VMEM((local, rows), BF16),
            pltpu.VMEM((local, rows), BF16),
            pltpu.VMEM((local, 128), F32),
            pltpu.VMEM((-(-depth // 128) * 128, 128), F32),
            pltpu.VMEM((4, 8, rows), F32),
            pltpu.VMEM((rows, 128), F32),
            exchange,
            exchange,
            exchange,
            exchange,
            exchange,
            pltpu.VMEM((half, head), BF16),
            pltpu.VMEM((half, head), BF16),
            pltpu.VMEM((4, rows, head), BF16),
            pltpu.VMEM((rows, 128), F32),
            exchange,
            pieces,
            pieces,
            pltpu.VMEM((4, nz, depth, head), F32),
            pltpu.VMEM((4, 2, nz, depth, head), BF16),
            pltpu.VMEM((4, 2, nz, depth, head), BF16),
            dma((6,)),
            dma((4, 3, nz)),
            dma((4, n)),
            dma((4,)),
            dma((4,)),
            dma((4,)),
            dma((4,)),
            dma((4,)),
            dma((4,)),
            dma((5,)),
            dma((5,)),
            dma((4, nz)),
            dma((4, nz)),
            dma((4, 2, nz)),
            dma((4, 2, nz)),
        ],
        compiler_params=pltpu.CompilerParams(
            collective_id=0, has_side_effects=True, vmem_limit_bytes=50 * 1024 * 1024
        ),
        name="head_backward",
    )(tokens, grad_out, gain.reshape(1, local), qkv_weight, out_weight.T)


def on_device(tokens, grad_out, gain, qkv_weight, out_weight):
    tok_rows, local_width = tokens.shape
    model_width = local_width * lax.axis_size("sec")
    head_size = out_weight.shape[0]
    shards = lax.axis_size("fsdp")
    depth = qkv_weight.shape[0]
    if depth % 64 or tok_rows != 2 * PATCHES or lax.axis_size("sec") != 4 or shards % 2:
        return by_collectives(tokens, grad_out, gain, qkv_weight, out_weight)
    grad_tokens, grads, grad_gain = fused(
        shards // 2, model_width, tokens, grad_out, gain, qkv_weight, out_weight
    )
    return grad_tokens, grads[:, head_size:], grads[:, :head_size].T, grad_gain.reshape(depth)


def by_collectives(tokens, grad_out, gain, qkv_weight, out_weight):
    tok_rows, local_width = tokens.shape
    model_width = local_width * lax.axis_size("sec")
    head_size = out_weight.shape[0]
    images = tok_rows // PATCHES
    tok_float = tokens.astype(jnp.float32)
    row_sums, row_squares = lax.psum(
        (jnp.sum(tok_float, axis=1), jnp.sum(tok_float * tok_float, axis=1)), "sec"
    )
    row_mean = row_sums / model_width
    row_var = row_squares / model_width - row_mean * row_mean
    inv_std = lax.rsqrt(row_var + EPS)
    normed = (tok_float - row_mean[:, None]) * inv_std[:, None]
    hidden = (normed * gain[None, :]).astype(jnp.bfloat16)
    columns = hidden
    partial_value = jnp.dot(
        columns,
        lax.all_gather(qkv_weight, "fsdp", axis=0, tiled=True),
        preferred_element_type=jnp.float32,
    )
    proj = lax.psum(partial_value, "sec").astype(jnp.bfloat16)
    parts = proj.reshape(images, PATCHES, 3, head_size)
    query, key_in, value = (parts[:, :, 0], parts[:, :, 1], parts[:, :, 2])
    scale = 1.0 / head_size**0.5
    scores = jnp.einsum("ipd,iqd->ipq", query, key_in, preferred_element_type=jnp.float32) * scale
    probs = jax.nn.softmax(scores, axis=-1)
    probs_b = probs.astype(jnp.bfloat16)
    attended = jnp.einsum(
        "ipq,iqd->ipd", probs_b, value, preferred_element_type=jnp.float32
    ).astype(jnp.bfloat16)
    attended = attended.reshape(tok_rows, head_size)
    local_outw = lax.dot_general(
        attended, grad_out, (((0,), (0,)), ((), ())), preferred_element_type=jnp.float32
    )
    grad_outw = lax.psum_scatter(local_outw, "fsdp", scatter_dimension=1, tiled=True)
    columns = grad_out
    att_partial = lax.dot_general(
        columns,
        lax.all_gather(out_weight, "fsdp", axis=1, tiled=True),
        (((1,), (1,)), ((), ())),
        preferred_element_type=jnp.float32,
    )
    grad_att = lax.psum(att_partial, "sec").astype(jnp.bfloat16)
    grad_att3 = grad_att.reshape(images, PATCHES, head_size)
    grad_prob = jnp.einsum("ipd,iqd->ipq", grad_att3, value, preferred_element_type=jnp.float32)
    grad_score = (
        probs * (grad_prob - jnp.sum(grad_prob * probs, axis=-1, keepdims=True)) * scale
    ).astype(jnp.bfloat16)
    grad_query = jnp.einsum("ipq,iqd->ipd", grad_score, key_in, preferred_element_type=jnp.float32)
    grad_key = jnp.einsum("ipq,ipd->iqd", grad_score, query, preferred_element_type=jnp.float32)
    grad_value = jnp.einsum("ipq,ipd->iqd", probs_b, grad_att3, preferred_element_type=jnp.float32)
    grad_proj = (
        jnp.stack([grad_query, grad_key, grad_value], axis=2)
        .reshape(tok_rows, 3 * head_size)
        .astype(jnp.bfloat16)
    )
    local_qkv = lax.dot_general(
        hidden, grad_proj, (((0,), (0,)), ((), ())), preferred_element_type=jnp.float32
    )
    grad_hidden = lax.dot_general(
        grad_proj,
        lax.all_gather(qkv_weight, "fsdp", axis=0, tiled=True),
        (((1,), (1,)), ((), ())),
        preferred_element_type=jnp.float32,
    )
    local_gain = jnp.sum(grad_hidden * normed, axis=0)
    grad_normed = grad_hidden * gain[None, :]
    first_sum, second_sum = lax.psum(
        (jnp.sum(grad_normed, axis=1), jnp.sum(grad_normed * normed, axis=1)), "sec"
    )
    first = first_sum / model_width
    second = second_sum / model_width
    grad_tokens = grad_out.astype(jnp.float32) + inv_std[:, None] * (
        grad_normed - first[:, None] - normed * second[:, None]
    )
    grad_qkv, grad_gain = (
        lax.psum_scatter(local_qkv, "fsdp", scatter_dimension=0, tiled=True),
        lax.psum_scatter(local_gain, "fsdp", scatter_dimension=0, tiled=True),
    )
    return (grad_tokens.astype(jnp.bfloat16), grad_qkv, grad_outw, grad_gain)


def solution(mesh):
    placed = (
        P("fsdp", "sec"),
        P("fsdp", "sec"),
        P("sec"),
        P(("sec", "fsdp"), None),
        P(None, ("sec", "fsdp")),
    )
    return jax.shard_map(
        on_device,
        mesh=mesh,
        in_specs=placed,
        out_specs=(
            P("fsdp", "sec"),
            P(("sec", "fsdp"), None),
            P(None, ("sec", "fsdp")),
            P(("sec", "fsdp")),
        ),
        check_vma=False,
    )
```

```python
import functools

import jax
import jax.numpy as jnp
from jax import lax
from jax.experimental import pallas as pl
from jax.experimental.pallas import tpu as pltpu
from jax.sharding import PartitionSpec as P

PATCHES = 256
EPS = 1e-06
MESH = pl.DeviceIdType.MESH
F32 = jnp.float32
BF16 = jnp.bfloat16


def nn(a, b):
    return jnp.dot(a, b, preferred_element_type=F32)


def nt(a, b):
    return lax.dot_general(a, b, (((1,), (1,)), ((), ())), preferred_element_type=F32)


def tn(a, b):
    return lax.dot_general(a, b, (((0,), (0,)), ((), ())), preferred_element_type=F32)


def copy_to(src, dst, send, recv, device):
    return pltpu.make_async_remote_copy(
        src_ref=src,
        dst_ref=dst,
        send_sem=send,
        recv_sem=recv,
        device_id=device,
        device_id_type=MESH,
    )


def kernel(
    nz,
    width,
    tok_hbm,
    go_hbm,
    gain_ref,
    qkv_hbm,
    ow_hbm,
    gt_ref,
    grad_ref,
    ggain_ref,
    tok_ref,
    go_ref,
    weights,
    hidden,
    hidden_t,
    go_t,
    gain_t,
    gain_pad,
    stats,
    mean_inv,
    first_out,
    first_own,
    first_in,
    second_out,
    second_in,
    gp,
    moments,
    sums,
    y_out,
    y_in,
    own,
    chain_out,
    chain_in,
    load_sem,
    gather_send,
    gather_recv,
    stat_send,
    stat_recv,
    core_send,
    core_recv,
    x_send,
    x_recv,
    gp_send,
    gp_recv,
    y_send,
    y_recv,
    chain_send,
    chain_recv,
):
    rows, local = tok_ref.shape
    depth, head = ow_hbm.shape
    groups = weights.shape[0]
    half = rows // 2
    s = lax.axis_index("sec")
    f = lax.axis_index("fsdp")
    z, y = f // 2, f % 2
    c = s % 2
    core = {"sec": s + 1 - 2 * c}
    across = {"sec": (s + 2) % 4}
    other_y = {"fsdp": f + 1 - 2 * y}
    to_left = {"fsdp": f - 2}
    to_right = {"fsdp": f + 2}
    has_left = z > 0
    has_right = z < nz - 1

    barrier = pltpu.get_barrier_semaphore()

    def greet(device):
        pl.semaphore_signal(barrier, inc=1, device_id=device, device_id_type=MESH)

    greet(other_y)
    for k in range(1, 4):
        greet({"sec": (s + k) % 4})
    pl.when(has_left)(lambda: greet(to_left))
    pl.when(has_right)(lambda: greet(to_right))

    mine = pl.ds(pl.multiple_of(f * depth, depth), depth)
    loads = [pltpu.make_async_copy(ow_hbm, weights.at[0, mine, :], load_sem.at[0])]
    for g in range(1, groups):
        part_hbm = qkv_hbm.at[:, pl.ds((g - 1) * head, head)]
        loads.append(pltpu.make_async_copy(part_hbm, weights.at[g, mine, :], load_sem.at[g]))
    loads.append(pltpu.make_async_copy(tok_hbm, tok_ref, load_sem.at[4]))
    loads.append(pltpu.make_async_copy(go_hbm, go_ref, load_sem.at[5]))
    for load in loads:
        load.start()

    peers = 4 + has_left.astype(jnp.int32) + has_right.astype(jnp.int32)
    pl.semaphore_wait(barrier, peers)

    def block(g, shard):
        return weights.at[g, pl.ds(pl.multiple_of(shard * depth, depth), depth), :]

    def gather_copy(g, shard_z, way, device):
        shard = shard_z * 2 + y
        ref = block(g, shard)
        return copy_to(
            ref, ref, gather_send.at[g, way, shard_z], gather_recv.at[g, shard], device
        )

    def go_left(g, shard_z):
        return gather_copy(g, shard_z, 0, to_left)

    def go_right(g, shard_z):
        return gather_copy(g, shard_z, 1, to_right)

    def go_y(g, shard_z):
        return gather_copy(g, shard_z, 2, other_y)

    def arrived(g, shard):
        ref = block(g, shard)
        copy_to(
            ref, ref, gather_send.at[g, 0, 0], gather_recv.at[g, shard], other_y
        ).wait_recv()

    def send_own(g):
        pl.when(has_left)(lambda: go_left(g, z).start())
        pl.when(has_right)(lambda: go_right(g, z).start())
        go_y(g, z).start()

    def forward(g, d):
        @pl.when(z - d >= 0)
        def _():
            arrived(g, (z - d) * 2 + y)
            pl.when(has_right)(lambda: go_right(g, z - d).start())
            go_y(g, z - d).start()

        @pl.when(z + d < nz)
        def _():
            arrived(g, (z + d) * 2 + y)
            pl.when(has_left)(lambda: go_left(g, z + d).start())
            go_y(g, z + d).start()

    turn_order = (1, 2, 3, 0)

    def wave(w):
        for g_at, g in enumerate(turn_order):
            if 1 <= w - g_at < nz:
                forward(g, w - g_at)

    def gathered(g):
        for shard_z in range(nz):
            arrived(g, shard_z * 2 + 1 - y)

    def gather_sent():
        for g in range(groups):
            for shard_z in range(nz):
                pl.when(has_left & (z <= shard_z))(lambda: go_left(g, shard_z).wait_send())
                pl.when(has_right & (z >= shard_z))(lambda: go_right(g, shard_z).wait_send())
                go_y(g, shard_z).wait_send()

    loads[1].wait()
    send_own(1)
    loads[2].wait()
    send_own(2)
    loads[4].wait()

    step = 64
    lane = lax.broadcasted_iota(jnp.int32, (step, 128), 1)

    def row_sums(i, carry):
        r = pl.ds(pl.multiple_of(i * step, step), step)
        t = tok_ref[r, :].astype(F32)
        a = jnp.sum(t, axis=1, keepdims=True)
        b = jnp.sum(t * t, axis=1, keepdims=True)
        mean_inv[r, :] = jnp.where(lane == 0, a, b)
        return carry

    lax.fori_loop(0, rows // step, row_sums, 0)
    stats[s] = mean_inv[...].T[:8, :]

    def stat_copy(k):
        return copy_to(
            stats.at[s], stats.at[s], stat_send.at[k], stat_recv.at[s], {"sec": (s + k) % 4}
        )

    for k in range(1, 4):
        stat_copy(k).start()

    wave(1)
    loads[3].wait()
    send_own(3)
    wave(2)
    loads[0].wait()
    send_own(0)
    wave(3)
    loads[5].wait()

    tstep = 256

    def turn(src, dst):
        for i in range(rows // tstep):

            def body(j, carry):
                cols = pl.ds(pl.multiple_of(j * tstep, tstep), tstep)
                part = src[i * tstep : (i + 1) * tstep, cols].astype(F32)
                dst[cols, i * tstep : (i + 1) * tstep] = part.T.astype(BF16)
                return carry

            lax.fori_loop(0, local // tstep, body, 0)


    gain_row = gain_ref[...]
    g_hi = gain_row.astype(BF16)
    rest = gain_row - g_hi.astype(F32)
    g_mid = rest.astype(BF16)
    g_lo = (rest - g_mid.astype(F32)).astype(BF16)
    row16 = lax.broadcasted_iota(jnp.int32, (16, local), 0)
    gain16 = jnp.where(
        row16 == 0,
        g_hi.astype(F32),
        jnp.where(row16 == 1, g_mid.astype(F32), jnp.where(row16 == 2, g_lo.astype(F32), 0.0)),
    ).astype(BF16)

    my_rows = pl.ds(pl.multiple_of(c * half, half), half)
    their_rows = pl.ds(pl.multiple_of((1 - c) * half, half), half)

    def core_copy(g):
        return copy_to(
            first_out.at[g], first_in.at[g], core_send.at[g], core_recv.at[g], core
        )

    def x_copy(g):
        return copy_to(
            second_out.at[g], second_in.at[g], x_send.at[g], x_recv.at[g], across
        )

    def project(g, left):
        w = weights[g]
        u = jnp.sum(nn(gain16, w), axis=0, keepdims=True)
        u = jnp.broadcast_to(u, (8, head))
        first_out[g, half : half + 8, :] = u
        first_out[g, 0:half, :] = nn(left[their_rows, :], w)
        core_copy(g).start()
        first_own[g, half : half + 8, :] = u
        first_own[g, 0:half, :] = nn(left[my_rows, :], w)

    def across_start(g):
        core_copy(g).wait_recv()
        second_out[g] = first_own[g] + first_in[g]
        x_copy(g).start()


    for k in range(1, 4):
        sender = (s + k) % 4
        copy_to(
            stats.at[sender], stats.at[sender], stat_send.at[k], stat_recv.at[sender], core
        ).wait_recv()
    total = stats[0] + stats[1] + stats[2] + stats[3]
    row_mean = total[0:1, :] / width
    row_var = total[1:2, :] / width - row_mean * row_mean
    inv_std = lax.rsqrt(row_var + EPS)
    sub = lax.broadcasted_iota(jnp.int32, (128, rows), 0)
    mean_inv[...] = jnp.where(sub == 0, row_mean, inv_std).T

    def norm(i, carry):
        r = pl.ds(pl.multiple_of(i * step, step), step)
        t = tok_ref[r, :].astype(F32)
        m = mean_inv[r, :]
        normed = (t - m[:, 0:1]) * m[:, 1:2]
        hidden[r, :] = (normed * gain_ref[...]).astype(BF16)
        return carry

    lax.fori_loop(0, rows // step, norm, 0)

    wave(4)
    gathered(1)
    project(1, hidden)
    wave(5)
    across_start(1)
    for w in range(6, nz + len(turn_order) - 1):
        wave(w)
    gathered(2)
    project(2, hidden)
    turn(go_ref, go_t)
    across_start(2)
    gathered(3)
    project(3, hidden)
    turn(hidden, hidden_t)
    across_start(3)
    gain_t[...] = jnp.broadcast_to(gain_ref[...], (128, local)).T
    gathered(0)
    project(0, go_ref)

    def finish(g):
        x_copy(g).wait_recv()
        sums[g] = second_out[g] + second_in[g]
        return sums[g, 0:half, :].astype(BF16)

    scale = 1.0 / head**0.5
    query = finish(1)
    key = finish(2)
    scores = nt(query, key) * scale
    e = jnp.exp(scores - jnp.max(scores, axis=-1, keepdims=True))
    probs = e / jnp.sum(e, axis=-1, keepdims=True)
    probs_b = probs.astype(BF16)
    across_start(0)

    def gp_piece(k, r):
        return moments.at[r, :] if k == groups else gp.at[k, r, :]

    def gp_copy(k):
        ref = gp_piece(k, my_rows)
        return copy_to(ref, ref, gp_send.at[k], gp_recv.at[k], core)

    def gp_arrived(k):
        ref = gp_piece(k, their_rows)
        copy_to(ref, ref, gp_send.at[k], gp_recv.at[k], core).wait_recv()

    def gp_put(k, result):
        rounded = result.astype(BF16)
        gp[k, my_rows, :] = rounded
        gp_copy(k).start()
        return rounded

    value = finish(3)
    gp_put(0, nn(probs_b, value))

    def span(g):
        return slice(g * head, (g + 1) * head)

    near = (z < nz // 2).astype(jnp.int32)

    def far_end(way, k):
        return way * (nz - 1 - k) + (1 - way) * k

    def part(g, shard):
        r = pl.ds(pl.multiple_of(shard * depth, depth), depth)
        return nn((go_t if g == 0 else hidden_t)[r, :], gp[g])

    def y_copy(g, shard_z):
        return copy_to(
            y_out.at[g, shard_z],
            y_in.at[g, shard_z],
            y_send.at[g, shard_z],
            y_recv.at[g, shard_z],
            other_y,
        )

    def y_phase(g):
        gp_arrived(g)
        for k in range(nz):
            shard_z = far_end(near, k)
            y_out[g, shard_z] = part(g, shard_z * 2 + 1 - y).astype(BF16)
            y_copy(g, shard_z).start()

    def own_phase(g):
        for k in range(nz):
            own[g, k] = part(g, k * 2 + y)

    def chain_copy(g, way, dest):
        return copy_to(
            chain_out.at[g, way, dest],
            chain_in.at[g, way, dest],
            chain_send.at[g, way, dest],
            chain_recv.at[g, way, dest],
            {"fsdp": f + 4 * way - 2},
        )

    def chain(g, leg):
        way = near if leg == 0 else 1 - near
        follows = ((way == 1) & has_left) | ((way == 0) & has_right)
        for k in range(nz - 1):
            dest = far_end(way, k)
            passes = ((way == 1) & (dest > z)) | ((way == 0) & (dest < z))

            @pl.when(passes)
            def _():
                y_copy(g, dest).wait_recv()
                here = own[g, dest] + y_in[g, dest].astype(F32)

                @pl.when(follows)
                def _():
                    chain_copy(g, way, dest).wait_recv()
                    chain_out[g, way, dest] = (
                        here + chain_in[g, way, dest].astype(F32)
                    ).astype(BF16)

                @pl.when(jnp.logical_not(follows))
                def _():
                    chain_out[g, way, dest] = here.astype(BF16)

                chain_copy(g, way, dest).start()

    def chain_end(g):
        y_copy(g, z).wait_recv()
        grad_ref[:, span(g)] = own[g, z] + y_in[g, z].astype(F32)

        @pl.when(has_left)
        def _():
            chain_copy(g, 1, z).wait_recv()
            grad_ref[:, span(g)] += chain_in[g, 1, z].astype(F32)

        @pl.when(has_right)
        def _():
            chain_copy(g, 0, z).wait_recv()
            grad_ref[:, span(g)] += chain_in[g, 0, z].astype(F32)

        if g == 0:
            return 0.0
        held = weights[g, mine, :].astype(F32)
        return jnp.sum(held * grad_ref[:, span(g)], axis=1, keepdims=True)

    y_phase(0)

    grad_att = finish(0)
    grad_value = gp_put(3, tn(probs_b, grad_att))
    grad_prob = nt(grad_att, value)
    grad_score = (
        probs * (grad_prob - jnp.sum(grad_prob * probs, axis=-1, keepdims=True)) * scale
    ).astype(BF16)
    y_phase(3)
    grad_query = gp_put(1, nn(grad_score, key))
    grad_key = gp_put(2, tn(grad_score, query))
    lane_h = lax.broadcasted_iota(jnp.int32, (half, 128), 1)
    first = jnp.zeros((half, 1), F32)
    second = jnp.zeros((half, 1), F32)
    for g, grad in ((1, grad_query), (2, grad_key), (3, grad_value)):
        r32 = grad.astype(F32)
        u = sums[g, half : half + 1, :]
        first += jnp.sum(r32 * u, axis=1, keepdims=True)
        second += jnp.sum(r32 * sums[g, 0:half, :], axis=1, keepdims=True)
    moments[my_rows, :] = jnp.where(lane_h == 0, first, second) / width
    gp_copy(groups).start()

    tile = 256

    def token_tile(j):
        cols = pl.ds(pl.multiple_of(j * tile, tile), tile)
        grad_hidden = nt(gp[1], weights[1, cols, :])
        for g in range(2, groups):
            grad_hidden += nt(gp[g], weights[g, cols, :])
        m = mean_inv[...]
        inv = m[:, 1:2]
        normed = (tok_ref[:, cols].astype(F32) - m[:, 0:1]) * inv
        mo = moments[...]
        grad_normed = grad_hidden * gain_ref[:, cols]
        gt_ref[:, cols] = (
            go_ref[:, cols].astype(F32)
            + inv * (grad_normed - mo[:, 0:1] - normed * mo[:, 1:2])
        ).astype(BF16)

    tiles = local // tile
    y_phase(1)
    y_phase(2)
    cuts = [tiles * k // 3 for k in range(4)]

    def some_tiles(k):
        for j in range(cuts[k], cuts[k + 1]):
            token_tile(j)

    own_phase(0)
    chain(0, 0)
    own_phase(3)
    chain(0, 1)
    gp_arrived(groups)
    some_tiles(0)
    chain(3, 0)
    own_phase(1)
    chain_end(0)
    some_tiles(1)
    chain(1, 0)
    chain(3, 1)
    own_phase(2)
    gain_sum = chain_end(3)
    chain(2, 0)
    chain(1, 1)
    some_tiles(2)
    chain(2, 1)
    gain_sum += chain_end(1)
    gain_sum += chain_end(2)
    gain_pad[...] = jnp.zeros_like(gain_pad)
    gain_pad[0:depth, :] = gain_sum / gain_t[mine, :]
    ggain_ref[...] = gain_pad[...].T[0:1, 0:depth]

    gather_sent()
    for k in range(1, 4):
        stat_copy(k).wait_send()
    for g in range(groups):
        core_copy(g).wait_send()
        x_copy(g).wait_send()
    for k in range(groups + 1):
        gp_copy(k).wait_send()
    for g in range(groups):
        for k in range(nz):
            y_copy(g, k).wait_send()
            pl.when(z > k)(lambda: chain_copy(g, 0, k).wait_send())
            pl.when(z < k)(lambda: chain_copy(g, 1, k).wait_send())


def fused(nz, width, tokens, grad_out, gain, qkv_weight, out_weight):
    rows, local = tokens.shape
    head = out_weight.shape[0]
    depth = qkv_weight.shape[0]
    half = rows // 2
    n = 2 * nz
    vmem = pl.BlockSpec(memory_space=pltpu.VMEM)
    hbm = pl.BlockSpec(memory_space=pltpu.HBM)
    dma = pltpu.SemaphoreType.DMA
    exchange = pltpu.VMEM((4, half + 8, head), F32)
    pieces = pltpu.VMEM((4, nz, depth, head), BF16)
    return pl.pallas_call(
        functools.partial(kernel, nz, width),
        out_shape=(
            jax.ShapeDtypeStruct((rows, local), BF16),
            jax.ShapeDtypeStruct((depth, 4 * head), F32),
            jax.ShapeDtypeStruct((1, depth), F32),
        ),
        in_specs=[hbm, hbm, vmem, hbm, hbm],
        out_specs=(vmem, vmem, vmem),
        scratch_shapes=[
            pltpu.VMEM((rows, local), BF16),
            pltpu.VMEM((rows, local), BF16),
            pltpu.VMEM((4, local, head), BF16),
            pltpu.VMEM((rows, local), BF16),
            pltpu.VMEM((local, rows), BF16),
            pltpu.VMEM((local, rows), BF16),
            pltpu.VMEM((local, 128), F32),
            pltpu.VMEM((-(-depth // 128) * 128, 128), F32),
            pltpu.VMEM((4, 8, rows), F32),
            pltpu.VMEM((rows, 128), F32),
            exchange,
            exchange,
            exchange,
            exchange,
            exchange,
            pltpu.VMEM((4, rows, head), BF16),
            pltpu.VMEM((rows, 128), F32),
            exchange,
            pieces,
            pieces,
            pltpu.VMEM((4, nz, depth, head), F32),
            pltpu.VMEM((4, 2, nz, depth, head), BF16),
            pltpu.VMEM((4, 2, nz, depth, head), BF16),
            dma((6,)),
            dma((4, 3, nz)),
            dma((4, n)),
            dma((4,)),
            dma((4,)),
            dma((4,)),
            dma((4,)),
            dma((4,)),
            dma((4,)),
            dma((5,)),
            dma((5,)),
            dma((4, nz)),
            dma((4, nz)),
            dma((4, 2, nz)),
            dma((4, 2, nz)),
        ],
        compiler_params=pltpu.CompilerParams(
            collective_id=0, has_side_effects=True, vmem_limit_bytes=50 * 1024 * 1024
        ),
        name="head_backward",
    )(tokens, grad_out, gain.reshape(1, local), qkv_weight, out_weight.T)


def on_device(tokens, grad_out, gain, qkv_weight, out_weight):
    tok_rows, local_width = tokens.shape
    model_width = local_width * lax.axis_size("sec")
    head_size = out_weight.shape[0]
    shards = lax.axis_size("fsdp")
    depth = qkv_weight.shape[0]
    if depth % 64 or tok_rows != 2 * PATCHES or lax.axis_size("sec") != 4 or shards % 2:
        return by_collectives(tokens, grad_out, gain, qkv_weight, out_weight)
    grad_tokens, grads, grad_gain = fused(
        shards // 2, model_width, tokens, grad_out, gain, qkv_weight, out_weight
    )
    return grad_tokens, grads[:, head_size:], grads[:, :head_size].T, grad_gain.reshape(depth)


def by_collectives(tokens, grad_out, gain, qkv_weight, out_weight):
    tok_rows, local_width = tokens.shape
    model_width = local_width * lax.axis_size("sec")
    head_size = out_weight.shape[0]
    images = tok_rows // PATCHES
    tok_float = tokens.astype(jnp.float32)
    row_sums, row_squares = lax.psum(
        (jnp.sum(tok_float, axis=1), jnp.sum(tok_float * tok_float, axis=1)), "sec"
    )
    row_mean = row_sums / model_width
    row_var = row_squares / model_width - row_mean * row_mean
    inv_std = lax.rsqrt(row_var + EPS)
    normed = (tok_float - row_mean[:, None]) * inv_std[:, None]
    hidden = (normed * gain[None, :]).astype(jnp.bfloat16)
    columns = hidden
    partial_value = jnp.dot(
        columns,
        lax.all_gather(qkv_weight, "fsdp", axis=0, tiled=True),
        preferred_element_type=jnp.float32,
    )
    proj = lax.psum(partial_value, "sec").astype(jnp.bfloat16)
    parts = proj.reshape(images, PATCHES, 3, head_size)
    query, key_in, value = (parts[:, :, 0], parts[:, :, 1], parts[:, :, 2])
    scale = 1.0 / head_size**0.5
    scores = jnp.einsum("ipd,iqd->ipq", query, key_in, preferred_element_type=jnp.float32) * scale
    probs = jax.nn.softmax(scores, axis=-1)
    probs_b = probs.astype(jnp.bfloat16)
    attended = jnp.einsum(
        "ipq,iqd->ipd", probs_b, value, preferred_element_type=jnp.float32
    ).astype(jnp.bfloat16)
    attended = attended.reshape(tok_rows, head_size)
    local_outw = lax.dot_general(
        attended, grad_out, (((0,), (0,)), ((), ())), preferred_element_type=jnp.float32
    )
    grad_outw = lax.psum_scatter(local_outw, "fsdp", scatter_dimension=1, tiled=True)
    columns = grad_out
    att_partial = lax.dot_general(
        columns,
        lax.all_gather(out_weight, "fsdp", axis=1, tiled=True),
        (((1,), (1,)), ((), ())),
        preferred_element_type=jnp.float32,
    )
    grad_att = lax.psum(att_partial, "sec").astype(jnp.bfloat16)
    grad_att3 = grad_att.reshape(images, PATCHES, head_size)
    grad_prob = jnp.einsum("ipd,iqd->ipq", grad_att3, value, preferred_element_type=jnp.float32)
    grad_score = (
        probs * (grad_prob - jnp.sum(grad_prob * probs, axis=-1, keepdims=True)) * scale
    ).astype(jnp.bfloat16)
    grad_query = jnp.einsum("ipq,iqd->ipd", grad_score, key_in, preferred_element_type=jnp.float32)
    grad_key = jnp.einsum("ipq,ipd->iqd", grad_score, query, preferred_element_type=jnp.float32)
    grad_value = jnp.einsum("ipq,ipd->iqd", probs_b, grad_att3, preferred_element_type=jnp.float32)
    grad_proj = (
        jnp.stack([grad_query, grad_key, grad_value], axis=2)
        .reshape(tok_rows, 3 * head_size)
        .astype(jnp.bfloat16)
    )
    local_qkv = lax.dot_general(
        hidden, grad_proj, (((0,), (0,)), ((), ())), preferred_element_type=jnp.float32
    )
    grad_hidden = lax.dot_general(
        grad_proj,
        lax.all_gather(qkv_weight, "fsdp", axis=0, tiled=True),
        (((1,), (1,)), ((), ())),
        preferred_element_type=jnp.float32,
    )
    local_gain = jnp.sum(grad_hidden * normed, axis=0)
    grad_normed = grad_hidden * gain[None, :]
    first_sum, second_sum = lax.psum(
        (jnp.sum(grad_normed, axis=1), jnp.sum(grad_normed * normed, axis=1)), "sec"
    )
    first = first_sum / model_width
    second = second_sum / model_width
    grad_tokens = grad_out.astype(jnp.float32) + inv_std[:, None] * (
        grad_normed - first[:, None] - normed * second[:, None]
    )
    grad_qkv, grad_gain = (
        lax.psum_scatter(local_qkv, "fsdp", scatter_dimension=0, tiled=True),
        lax.psum_scatter(local_gain, "fsdp", scatter_dimension=0, tiled=True),
    )
    return (grad_tokens.astype(jnp.bfloat16), grad_qkv, grad_outw, grad_gain)


def solution(mesh):
    placed = (
        P("fsdp", "sec"),
        P("fsdp", "sec"),
        P("sec"),
        P(("sec", "fsdp"), None),
        P(None, ("sec", "fsdp")),
    )
    return jax.shard_map(
        on_device,
        mesh=mesh,
        in_specs=placed,
        out_specs=(
            P("fsdp", "sec"),
            P(("sec", "fsdp"), None),
            P(None, ("sec", "fsdp")),
            P(("sec", "fsdp")),
        ),
        check_vma=False,
    )
```
